32 devices in a mesh: blk: 16 (over z, y, core), group: 2 (over x).
Axes of the slice: x: 2, y: 2, z: 4, core: 2. Of those that a mesh axis runs over, the one named last changes fastest.
Arguments:
- image_feats: bfloat16 [4096, 768], P(('blk', 'group')), may hold values from -0.796875 to 0.796875
- text_feats: bfloat16 [4096, 768], P(('blk', 'group')), may hold values from -0.796875 to 0.796875
- image_proj: bfloat16 [768, 768], replicated, may hold values from -0.21875 to 0.21875
- text_proj: bfloat16 [768, 768], replicated, may hold values from -0.21875 to 0.21875
- logit_scale: float32 [1], replicated, may hold values from 5 to 20
- logit_bias: float32 [1], replicated, may hold values from -3 to 0
- match: int32 [4096], P(('blk', 'group')), may hold values from 0 to 4095, as said below
Outputs:
- grad_image_feats: bfloat16 [4096, 768], P(('blk', 'group'))
- grad_text_feats: bfloat16 [4096, 768], P(('blk', 'group'))
The draws below stay inside these ranges and needn't reach their ends.
Inputs may be any that keep to these rules, and one draw needn't show every extreme that they name: match of an image row in block b (rows b * 2 * 128 to (b + 1) * 2 * 128 - 1) names a report row of one of the blocks (b - k) mod 16, k below 4.
All inputs are finite; a program needn't handle non-finite values.
Results may differ from the reference program's by a relative error of at most 0.02.
Values may be sent and summed in bfloat16 or wider, within the bound.
A program may use at most 64 MiB of HBM per device.

```python
import math
import jax
import jax.numpy as jnp
from jax import lax

D = 768
ROWS = 128
SPAN = 4
IMAGES = 4096
N_BLK = 16
N_GROUP = 2


def draw_match(key, part):
    key = jax.random.fold_in(key, 11)
    total = ROWS * N_GROUP * N_BLK
    first, second, third = jax.random.split(key, 3)
    row_ids = jnp.arange(total, dtype=jnp.int32)
    block = row_ids // (N_GROUP * ROWS)
    back = jax.random.randint(first, (total,), 0, SPAN, dtype=jnp.int32)
    side = jax.random.randint(second, (total,), 0, N_GROUP, dtype=jnp.int32)
    offset = jax.random.randint(third, (total,), 0, ROWS, dtype=jnp.int32)
    back = jnp.where(row_ids == 0, jnp.int32(1), jnp.where(row_ids == 1, jnp.int32(0), back))
    side = jnp.where(row_ids == 0, jnp.int32(N_GROUP - 1), jnp.where(row_ids == 1, jnp.int32(0), side))
    offset = jnp.where(row_ids == 0, jnp.int32(ROWS - 1), jnp.where(row_ids == 1, jnp.int32(0), offset))
    return (((block - back) % N_BLK * N_GROUP + side) * ROWS + offset).astype(jnp.int32)


def block_scale(rng, shape, cuts, low, high):
    def one(position, parts):
        steps = jax.random.uniform(jax.random.fold_in(jax.random.fold_in(rng, 6), position), (parts,), jnp.float32, low / len(cuts), high / len(cuts))
        return jnp.repeat(jnp.exp(steps), shape[position] // parts).reshape((-1,) + (1,) * (len(shape) - position - 1))

    loudness = one(*cuts[0])
    for cut in cuts[1:]:
        loudness = loudness * one(*cut)
    return loudness


def scatter_about(stream_key, dims, scale, bound, pieces=(), kind=jnp.bfloat16):
    result = scale * jax.random.normal(stream_key, dims, jnp.float32)
    if pieces:
        result = result * block_scale(stream_key, dims, pieces, -0.22, 0.18)
    return jnp.clip(result, -bound, bound).astype(kind)


def setup_inputs(seed: int = 0) -> dict:
    splits = jax.random.split(jax.random.key(seed), 8)
    return {
        "image_feats": scatter_about(splits[0], (IMAGES, D), 0.1, 0.796875, ((0, 32),)),
        "text_feats": scatter_about(splits[1], (IMAGES, D), 0.1, 0.796875, ((0, 32),)),
        "image_proj": scatter_about(splits[2], (D, D), D ** -0.5, 0.21875),
        "text_proj": scatter_about(splits[3], (D, D), D ** -0.5, 0.21875),
        "logit_scale": jnp.clip(jnp.exp(jax.random.uniform(splits[4], (1,), jnp.float32, math.log(5.0), math.log(20.0))), 5.0, 20.0),
        "logit_bias": jnp.clip(jax.random.uniform(splits[5], (1,), jnp.float32, -3.0, 0.0), -3.0, 0.0),
        "match": draw_match(jax.random.fold_in(splits[7], 71), 0),
    }


def embed(feats, proj):
    x = jnp.dot(feats, proj, preferred_element_type=jnp.float32)
    inv = lax.rsqrt(lax.optimization_barrier(jnp.sum(x * x, axis=-1, keepdims=True)) + 1e-06)
    return (x * inv, inv)

def back_norm(grad, unit, inv, proj):
    inner = lax.optimization_barrier(jnp.sum(grad * unit, axis=-1, keepdims=True))
    grad_x = (inv * (grad - inner * unit)).astype(jnp.bfloat16)
    out = lax.dot_general(grad_x, proj, (((1,), (1,)), ((), ())), preferred_element_type=jnp.float32)
    return out.astype(jnp.bfloat16)

def reference(image_feats, text_feats, image_proj, text_proj, logit_scale, logit_bias, match):
    image_unit, image_inv = embed(image_feats, image_proj)
    text_unit, text_inv = embed(text_feats, text_proj)
    width_rows = N_GROUP * ROWS
    image_emb = image_unit.astype(jnp.bfloat16).reshape(N_BLK, width_rows, D).astype(jnp.float32)
    text_emb = text_unit.astype(jnp.bfloat16).reshape(N_BLK, width_rows, D).astype(jnp.float32)
    match_blocks = match.reshape(N_BLK, width_rows)
    scale = logit_scale[0]
    bias = logit_bias[0]
    block_ids = jnp.arange(N_BLK, dtype=jnp.int32)
    local_ids = jnp.arange(width_rows, dtype=jnp.int32)
    grad_image = jnp.zeros((N_BLK, width_rows, D), jnp.float32)
    grad_text = jnp.zeros((N_BLK, width_rows, D), jnp.float32)
    for step in range(SPAN):
        visiting = jnp.roll(text_emb, step, axis=0)
        source = ((block_ids - step) % N_BLK).astype(jnp.int32)
        text_ids = source[:, None] * width_rows + local_ids[None, :]
        sign = jnp.where(match_blocks[:, :, None] == text_ids[:, None, :], jnp.float32(1.0), jnp.float32(-1.0))
        logits = scale * jnp.einsum('bid,bjd->bij', image_emb, visiting) + bias
        coef = (-sign * jax.nn.sigmoid(-sign * logits) * scale).astype(jnp.bfloat16).astype(jnp.float32)
        grad_image = grad_image + jnp.einsum('bij,bjd->bid', coef, visiting)
        term = jnp.einsum('bij,bid->bjd', coef, image_emb)
        grad_text = grad_text + jnp.roll(term, -step, axis=0)
    grad_image = grad_image.reshape(N_BLK * width_rows, D)
    grad_text = grad_text.reshape(N_BLK * width_rows, D)
    return (back_norm(grad_image, image_unit, image_inv, image_proj), back_norm(grad_text, text_unit, text_inv, text_proj))
```

```python
import functools

import jax
import jax.numpy as jnp
from jax import lax
from jax.experimental import pallas as pl
from jax.experimental.pallas import tpu as pltpu
from jax.sharding import PartitionSpec as P

MESH = pl.DeviceIdType.MESH
A, B, C, X, M, A2, B2, C2, X2 = range(9)


def embed(feats, proj):
    x = jnp.dot(feats, proj, preferred_element_type=jnp.float32)
    inv = lax.rsqrt(jnp.sum(x * x, axis=-1, keepdims=True) + 1e-06)
    return x * inv, inv


def back_norm(grad, unit, inv, proj):
    inner = jnp.sum(grad * unit, axis=-1, keepdims=True)
    grad_x = (inv * (grad - inner * unit)).astype(jnp.bfloat16)
    out = lax.dot_general(
        grad_x, proj, (((1,), (1,)), ((), ())), preferred_element_type=jnp.float32
    )
    return out.astype(jnp.bfloat16)


def kernel(
    n,
    image_feats, text_feats, image_proj, text_proj, scale_ref, bias_ref, match,
    image_out, text_out,
    feats_i, feats_t, proj_i, proj_t, out_i, out_t,
    unit_i, inv_i, unit_t, inv_t, images, text, match_nbr,
    text_a, text_b, text_c, gi, gt_own, gt_a, send_a, send_b, send_c, send_x,
    got_a, got_b, got_c, got_x,
    load_sem, store_sem, send_sem, recv_sem,
):
    rows = text.shape[0]
    blk = lax.axis_index("blk")
    grp = lax.axis_index("group")
    odd = lax.rem(blk, 2)

    def at(distance):
        return lax.rem(blk + distance + n, n)

    sibling = blk + 1 - 2 * odd
    across = (blk, 1 - grp)
    from_a, from_b, from_c = at(-2), at(2 * odd - 3), at(-1 - 2 * odd)

    loads = [
        pltpu.make_async_copy(src, dst, load_sem.at[i])
        for i, (src, dst) in enumerate(
            (
                (text_feats, feats_t),
                (text_proj, proj_t),
                (image_feats, feats_i),
                (image_proj, proj_i),
            )
        )
    ]
    for load in loads:
        load.start()

    barrier = pltpu.get_barrier_semaphore()
    for partner in (
        (at(2), grp), (at(-2), grp), (sibling, grp), (at(6 * odd - 3), grp), across
    ):
        pl.semaphore_signal(barrier, inc=1, device_id=partner, device_id_type=MESH)

    def remote(role, src, dst, partner):
        return pltpu.make_async_remote_copy(
            src_ref=src, dst_ref=dst, send_sem=send_sem.at[role],
            recv_sem=recv_sem.at[role], device_id=partner, device_id_type=MESH,
        )

    loads[0].wait()
    loads[1].wait()
    unit, inv = embed(feats_t[...], proj_t[...])
    unit_t[...] = unit
    inv_t[...] = inv
    text[...] = unit.astype(jnp.bfloat16)

    pl.semaphore_wait(barrier, 5)
    copy_a = remote(A, text, text_a, (at(2), grp))
    copy_b = remote(B, text, text_b, (at(1 + 2 * odd), grp))
    copy_m = remote(M, match, match_nbr, across)
    copy_a.start()
    copy_b.start()
    copy_m.start()

    loads[2].wait()
    loads[3].wait()
    unit, inv = embed(feats_i[...], proj_i[...])
    unit_i[...] = unit
    inv_i[...] = inv
    images[:rows, :] = unit.astype(jnp.bfloat16)
    copy_x = remote(X, images.at[pl.ds(0, rows)], images.at[pl.ds(rows, rows)], across)
    copy_x.start()

    scale = scale_ref[0]
    bias = bias_ref[0]

    def pair(texts, source):
        ids = (source * 2 + grp) * rows + lax.broadcasted_iota(
            jnp.int32, (rows, 2 * rows), 0
        )
        wanted = jnp.concatenate([match[...], match_nbr[...]], axis=1)
        hit = wanted == ids
        logits = (
            scale
            * lax.dot_general(
                texts, images[...], (((1,), (1,)), ((), ())),
                preferred_element_type=jnp.float32,
            )
            + bias
        )
        weight = jax.nn.sigmoid(jnp.where(hit, -logits, logits)) * scale
        coef = jnp.where(hit, -weight, weight).astype(jnp.bfloat16)
        term_t = jnp.dot(coef, images[...], preferred_element_type=jnp.float32)
        return coef, term_t

    def image_term(coef, texts):
        return lax.dot_general(
            coef, texts, (((0,), (0,)), ((), ())), preferred_element_type=jnp.float32
        )

    copy_m.wait()
    copy_x.wait()
    coef, term = pair(text[...], blk)
    gt_own[...] = term
    gi[...] = image_term(coef, text[...])

    copy_a.wait_recv()
    copy_c = remote(C, text_a, text_c, (sibling, grp))
    copy_c.start()
    coef, term = pair(text_a[...], from_a)
    gt_a[...] = term
    gi[...] += image_term(coef, text_a[...])

    copy_c.wait_recv()
    coef, term = pair(text_c[...], from_c)
    send_c[...] = term.astype(jnp.bfloat16)
    back_c = remote(C2, send_c, got_c, (sibling, grp))
    back_c.start()
    gi[...] += image_term(coef, text_c[...])

    copy_b.wait_recv()
    coef, term = pair(text_b[...], from_b)
    send_b[...] = term.astype(jnp.bfloat16)
    back_b = remote(B2, send_b, got_b, (from_b, grp))
    back_b.start()

    back_c.wait_recv()
    send_a[...] = (gt_a[...] + got_c[...].astype(jnp.float32)).astype(jnp.bfloat16)
    back_a = remote(A2, send_a, got_a, (from_a, grp))
    back_a.start()

    gi[...] += image_term(coef, text_b[...])
    send_x[...] = gi[rows:, :].astype(jnp.bfloat16)
    back_x = remote(X2, send_x, got_x, across)
    back_x.start()

    back_x.wait_recv()
    grad = gi[:rows, :] + got_x[...].astype(jnp.float32)
    out_i[...] = back_norm(grad, unit_i[...], inv_i[...], proj_i[...])
    store_i = pltpu.make_async_copy(out_i, image_out, store_sem.at[0])
    store_i.start()

    back_b.wait_recv()
    back_a.wait_recv()
    grad = gt_own[...] + got_a[...].astype(jnp.float32) + got_b[...].astype(jnp.float32)
    out_t[...] = back_norm(grad, unit_t[...], inv_t[...], proj_t[...])
    store_t = pltpu.make_async_copy(out_t, text_out, store_sem.at[1])
    store_t.start()

    for copy in (copy_a, copy_b, copy_c, back_a, back_b, back_c, back_x):
        copy.wait_send()
    store_i.wait()
    store_t.wait()


def body(image_feats, text_feats, image_proj, text_proj, logit_scale, logit_bias, match):
    n = lax.axis_size("blk")
    rows, depth = image_feats.shape
    half = lambda *shape: pltpu.VMEM(shape, jnp.bfloat16)
    full = lambda *shape: pltpu.VMEM(shape, jnp.float32)
    anywhere = pl.BlockSpec(memory_space=pl.ANY)
    scalar = pl.BlockSpec(memory_space=pltpu.SMEM)
    tile = (rows, depth)
    return pl.pallas_call(
        functools.partial(kernel, n),
        out_shape=[jax.ShapeDtypeStruct(tile, jnp.bfloat16)] * 2,
        in_specs=[anywhere] * 4 + [scalar] * 2 + [pl.BlockSpec(memory_space=pltpu.VMEM)],
        out_specs=[anywhere] * 2,
        scratch_shapes=[
            half(*tile), half(*tile), half(depth, depth), half(depth, depth),
            half(*tile), half(*tile),
            full(*tile), full(rows, 1), full(*tile), full(rows, 1),
            half(2 * rows, depth), half(*tile), pltpu.VMEM((1, rows), jnp.int32),
            half(*tile), half(*tile), half(*tile),
            full(2 * rows, depth), full(*tile), full(*tile),
            half(*tile), half(*tile), half(*tile), half(*tile),
            half(*tile), half(*tile), half(*tile), half(*tile),
            pltpu.SemaphoreType.DMA((4,)),
            pltpu.SemaphoreType.DMA((2,)),
            pltpu.SemaphoreType.DMA((9,)),
            pltpu.SemaphoreType.DMA((9,)),
        ],
        compiler_params=pltpu.CompilerParams(
            collective_id=0, has_side_effects=True, vmem_limit_bytes=32 * 1024 * 1024
        ),
        cost_estimate=pl.CostEstimate(
            flops=8 * rows * depth * depth + 48 * rows * rows * depth,
            bytes_accessed=4 * depth * depth + 8 * rows * depth,
            transcendentals=8 * rows * rows,
        ),
    )(
        image_feats, text_feats, image_proj, text_proj, logit_scale, logit_bias,
        match.reshape(1, rows),
    )


def solution(mesh):
    rows = P(("blk", "group"), None)
    return jax.shard_map(
        body,
        mesh=mesh,
        in_specs=(rows, rows, P(), P(), P(), P(), P(("blk", "group"))),
        out_specs=(rows, rows),
        check_vma=False,
    )
```

```python
import functools

import jax
import jax.numpy as jnp
from jax import lax
from jax.experimental import pallas as pl
from jax.experimental.pallas import tpu as pltpu
from jax.sharding import PartitionSpec as P

MESH = pl.DeviceIdType.MESH
SPAN = 4
OWN, AT_A, AT_C, AT_B = range(SPAN)
A, B, C, X, M, A2, B2, C2, X2 = range(9)


def embed(feats, proj):
    x = jnp.dot(feats, proj, preferred_element_type=jnp.float32)
    inv = lax.rsqrt(jnp.sum(x * x, axis=-1, keepdims=True) + 1e-06)
    return x * inv, inv


def back_norm(grad, unit, inv, turned):
    inner = jnp.sum(grad * unit, axis=-1, keepdims=True)
    grad_x = (inv * (grad - inner * unit)).astype(jnp.bfloat16)
    out = jnp.dot(grad_x, turned, preferred_element_type=jnp.float32)
    return out.astype(jnp.bfloat16)


def kernel(
    n,
    image_feats, text_feats, image_proj, text_proj, scale_ref, bias_ref, match,
    image_out, text_out,
    feats_i, feats_t, proj_i, proj_t, turned_i, turned_t,
    unit_i, inv_i, unit_t, inv_t, images, images_turned, texts, coefs, match_nbr,
    gt_own, gt_a, send_a, send_b, send_c, send_x,
    got_a, got_b, got_c, got_x,
    load_sem, send_sem, recv_sem,
):
    rows = match.shape[1]
    blk = lax.axis_index("blk")
    grp = lax.axis_index("group")
    odd = lax.rem(blk, 2)

    def at(distance):
        return lax.rem(blk + distance + n, n)

    sibling = blk + 1 - 2 * odd
    across = (blk, 1 - grp)
    from_a, from_b, from_c = at(-2), at(2 * odd - 3), at(-1 - 2 * odd)

    loads = [
        pltpu.make_async_copy(src, dst, load_sem.at[i])
        for i, (src, dst) in enumerate(
            (
                (text_feats, feats_t),
                (text_proj, proj_t),
                (image_feats, feats_i),
                (image_proj, proj_i),
            )
        )
    ]
    for load in loads:
        load.start()

    barrier = pltpu.get_barrier_semaphore()
    for partner in (
        (at(2), grp), (at(-2), grp), (sibling, grp), (at(6 * odd - 3), grp), across
    ):
        pl.semaphore_signal(barrier, inc=1, device_id=partner, device_id_type=MESH)

    def remote(role, src, dst, partner):
        return pltpu.make_async_remote_copy(
            src_ref=src, dst_ref=dst, send_sem=send_sem.at[role],
            recv_sem=recv_sem.at[role], device_id=partner, device_id_type=MESH,
        )

    def slot(place):
        return texts.at[pl.ds(place * rows, rows)]

    loads[0].wait()
    loads[1].wait()
    unit, inv = embed(feats_t[...], proj_t[...])
    texts[:rows, :] = unit.astype(jnp.bfloat16)

    pl.semaphore_wait(barrier, 5)
    copy_a = remote(A, slot(OWN), slot(AT_A), (at(2), grp))
    copy_b = remote(B, slot(OWN), slot(AT_B), (at(1 + 2 * odd), grp))
    copy_m = remote(M, match, match_nbr, across)
    copy_a.start()
    copy_b.start()
    copy_m.start()
    unit_t[...] = unit
    inv_t[...] = inv

    loads[2].wait()
    loads[3].wait()
    unit, inv = embed(feats_i[...], proj_i[...])
    images[:rows, :] = unit.astype(jnp.bfloat16)
    copy_x = remote(X, images.at[pl.ds(0, rows)], images.at[pl.ds(rows, rows)], across)
    copy_x.start()
    unit_i[...] = unit
    inv_i[...] = inv
    turned_t[...] = proj_t[...].T
    turned_i[...] = proj_i[...].T

    scale = scale_ref[0]
    bias = bias_ref[0]

    def pair(place, source):
        ids = (source * 2 + grp) * rows + lax.broadcasted_iota(
            jnp.int32, (rows, 2 * rows), 0
        )
        wanted = jnp.concatenate([match[...], match_nbr[...]], axis=1)
        hit = wanted == ids
        here = slice(place * rows, (place + 1) * rows)
        logits = (
            scale
            * jnp.dot(texts[here, :], images_turned[...], preferred_element_type=jnp.float32)
            + bias
        )
        weight = jax.nn.sigmoid(jnp.where(hit, -logits, logits)) * scale
        coef = jnp.where(hit, -weight, weight).astype(jnp.bfloat16)
        coefs[here, :] = coef
        return jnp.dot(coef, images[...], preferred_element_type=jnp.float32)

    def image_grad(which):
        return lax.dot_general(
            coefs[:, which], texts[...], (((0,), (0,)), ((), ())),
            preferred_element_type=jnp.float32,
        )

    copy_m.wait()
    copy_x.wait()
    images_turned[...] = images[...].T
    gt_own[...] = pair(OWN, blk)

    back_b = remote(B2, send_b, got_b, (from_b, grp))

    def finish_b():
        copy_b.wait_recv()
        send_b[...] = pair(AT_B, from_b).astype(jnp.bfloat16)
        back_b.start()

    pl.when(odd == 1)(finish_b)

    copy_a.wait_recv()
    copy_c = remote(C, slot(AT_A), slot(AT_C), (sibling, grp))
    copy_c.start()
    gt_a[...] = pair(AT_A, from_a)

    copy_c.wait_recv()
    send_c[...] = pair(AT_C, from_c).astype(jnp.bfloat16)
    back_c = remote(C2, send_c, got_c, (sibling, grp))
    back_c.start()

    back_c.wait_recv()
    send_a[...] = (gt_a[...] + got_c[...].astype(jnp.float32)).astype(jnp.bfloat16)
    back_a = remote(A2, send_a, got_a, (from_a, grp))
    back_a.start()

    pl.when(odd == 0)(finish_b)

    send_x[...] = image_grad(slice(rows, 2 * rows)).astype(jnp.bfloat16)
    back_x = remote(X2, send_x, got_x, across)
    back_x.start()
    grad = image_grad(slice(0, rows))

    back_x.wait_recv()
    grad = grad + got_x[...].astype(jnp.float32)
    image_out[...] = back_norm(grad, unit_i[...], inv_i[...], turned_i[...])

    back_b.wait_recv()
    grad = gt_own[...] + got_b[...].astype(jnp.float32)
    back_a.wait_recv()
    grad = grad + got_a[...].astype(jnp.float32)
    text_out[...] = back_norm(grad, unit_t[...], inv_t[...], turned_t[...])

    for copy in (copy_a, copy_b, copy_c, back_a, back_b, back_c, back_x):
        copy.wait_send()


def body(image_feats, text_feats, image_proj, text_proj, logit_scale, logit_bias, match):
    n = lax.axis_size("blk")
    rows, depth = image_feats.shape
    half = lambda *shape: pltpu.VMEM(shape, jnp.bfloat16)
    full = lambda *shape: pltpu.VMEM(shape, jnp.float32)
    far = pl.BlockSpec(memory_space=pltpu.HBM)
    near = pl.BlockSpec(memory_space=pltpu.VMEM)
    scalar = pl.BlockSpec(memory_space=pltpu.SMEM)
    tile = (rows, depth)
    return pl.pallas_call(
        functools.partial(kernel, n),
        out_shape=[jax.ShapeDtypeStruct(tile, jnp.bfloat16)] * 2,
        in_specs=[far] * 4 + [scalar] * 2 + [near],
        out_specs=[near] * 2,
        scratch_shapes=[
            half(*tile), half(*tile), half(depth, depth), half(depth, depth),
            half(depth, depth), half(depth, depth),
            full(*tile), full(rows, 1), full(*tile), full(rows, 1),
            half(2 * rows, depth), half(depth, 2 * rows),
            half(SPAN * rows, depth), half(SPAN * rows, 2 * rows),
            pltpu.VMEM((1, rows), jnp.int32),
            full(*tile), full(*tile),
            half(*tile), half(*tile), half(*tile), half(*tile),
            half(*tile), half(*tile), half(*tile), half(*tile),
            pltpu.SemaphoreType.DMA((4,)),
            pltpu.SemaphoreType.DMA((9,)),
            pltpu.SemaphoreType.DMA((9,)),
        ],
        compiler_params=pltpu.CompilerParams(
            collective_id=0, has_side_effects=True, vmem_limit_bytes=64 * 1024 * 1024
        ),
        cost_estimate=pl.CostEstimate(
            flops=8 * rows * depth * depth + 48 * rows * rows * depth,
            bytes_accessed=4 * depth * depth + 8 * rows * depth,
            transcendentals=8 * rows * rows,
        ),
    )(
        image_feats, text_feats, image_proj, text_proj, logit_scale, logit_bias,
        match.reshape(1, rows),
    )


def solution(mesh):
    rows = P(("blk", "group"), None)
    return jax.shard_map(
        body,
        mesh=mesh,
        in_specs=(rows, rows, P(), P(), P(), P(), P(("blk", "group"))),
        out_specs=(rows, rows),
        check_vma=False,
    )
```

```python
import functools

import jax
import jax.numpy as jnp
from jax import lax
from jax.experimental import pallas as pl
from jax.experimental.pallas import tpu as pltpu
from jax.sharding import PartitionSpec as P

MESH = pl.DeviceIdType.MESH
SPAN = 4
OWN, AT_A, AT_C, AT_B = range(SPAN)
CHUNKS = 2
A, B, C, R, A2, B2, C2, R2 = range(0, 8 * CHUNKS, CHUNKS)
X, M, X2 = range(8 * CHUNKS, 8 * CHUNKS + 3)
SEMS = 8 * CHUNKS + 3


def embed(feats, proj):
    x = jnp.dot(feats, proj, preferred_element_type=jnp.float32)
    inv = lax.rsqrt(jnp.sum(x * x, axis=-1, keepdims=True) + 1e-06)
    return x * inv, inv


def back_norm(grad, unit, inv, turned):
    inner = jnp.sum(grad * unit, axis=-1, keepdims=True)
    grad_x = (inv * (grad - inner * unit)).astype(jnp.bfloat16)
    out = jnp.dot(grad_x, turned, preferred_element_type=jnp.float32)
    return out.astype(jnp.bfloat16)


def kernel(
    n,
    image_feats, text_feats, image_proj, text_proj, scale_ref, bias_ref, match,
    out,
    feats_i, feats_t, proj_i, proj_t, turned_i, turned_t,
    unit_i, inv_i, unit_t, inv_t, images, images_turned, texts, coefs, match_nbr,
    gt_own, gt_a, gt_b, send_a, send_b, send_c, send_x,
    got_a, got_b, got_c, got_r, got_x,
    load_sem, send_sem, recv_sem,
):
    rows = match.shape[1]
    step = rows // CHUNKS
    blk = lax.axis_index("blk")
    grp = lax.axis_index("group")
    odd = lax.rem(blk, 2)
    q = lax.rem(blk, 4)

    def at(distance):
        return lax.rem(blk + distance + n, n)

    sibling = blk + 1 - 2 * odd
    across = (blk, 1 - grp)
    from_a, from_b, from_c = at(-2), at(2 * odd - 3), at(-1 - 2 * odd)

    loads = [
        pltpu.make_async_copy(src, dst, load_sem.at[i])
        for i, (src, dst) in enumerate(
            (
                (text_feats, feats_t),
                (text_proj, proj_t),
                (image_feats, feats_i),
                (image_proj, proj_i),
            )
        )
    ]
    for load in loads:
        load.start()

    barrier = pltpu.get_barrier_semaphore()

    def greet(partner):
        pl.semaphore_signal(barrier, inc=1, device_id=partner, device_id_type=MESH)

    greet((sibling, grp))
    greet(across)
    greet((at(6 * odd - 3), grp))
    pl.when(q != 3)(lambda: greet((at(2), grp)))
    pl.when(q != 1)(lambda: greet((at(-2), grp)))
    pl.when(q == 1)(lambda: greet((at(1), grp)))
    pl.when(q == 2)(lambda: greet((at(-1), grp)))

    def remote(send, recv, src, dst, partner):
        return pltpu.make_async_remote_copy(
            src_ref=src, dst_ref=dst, send_sem=send_sem.at[send],
            recv_sem=recv_sem.at[recv], device_id=partner, device_id_type=MESH,
        )

    def part(i):
        return pl.ds(i * step, step)

    def between(send, recv, src, dst, partner):
        return [
            remote(send + i, recv + i, src.at[part(i)], dst.at[part(i)], partner)
            for i in range(CHUNKS)
        ]

    def start(copies):
        for copy in copies:
            copy.start()

    def wait_recv(copies):
        for copy in copies:
            copy.wait_recv()

    def wait_send(copies):
        for copy in copies:
            copy.wait_send()

    def slot(place):
        return texts.at[pl.ds(place * rows, rows)]

    loads[0].wait()
    loads[1].wait()
    unit, inv = embed(feats_t[...], proj_t[...])
    texts[:rows, :] = unit.astype(jnp.bfloat16)

    pl.semaphore_wait(barrier, 5 + (q == 2).astype(jnp.int32) - (q == 3).astype(jnp.int32))
    copy_a = between(A, A, slot(OWN), slot(AT_A), (at(2), grp))
    copy_b = between(B, B, slot(OWN), slot(AT_B), (at(1 + 2 * odd), grp))
    copy_c = between(C, C, slot(AT_A), slot(AT_C), (sibling, grp))
    relay = between(R, A, slot(AT_B), slot(AT_A), (at(-1), grp))
    copy_m = remote(M, M, match, match_nbr, across)
    pl.when(q != 3)(lambda: start(copy_a))
    start(copy_b)
    copy_m.start()
    unit_t[...] = unit
    inv_t[...] = inv

    loads[2].wait()
    loads[3].wait()
    unit, inv = embed(feats_i[...], proj_i[...])
    images[:rows, :] = unit.astype(jnp.bfloat16)
    copy_x = remote(X, X, images.at[pl.ds(0, rows)], images.at[pl.ds(rows, rows)], across)
    copy_x.start()
    unit_i[...] = unit
    inv_i[...] = inv
    turned_t[...] = proj_t[...].T
    turned_i[...] = proj_i[...].T

    scale = scale_ref[0]
    bias = bias_ref[0]

    def pair(place, source):
        ids = (source * 2 + grp) * rows + lax.broadcasted_iota(
            jnp.int32, (rows, 2 * rows), 0
        )
        wanted = jnp.concatenate([match[...], match_nbr[...]], axis=1)
        hit = wanted == ids
        here = slice(place * rows, (place + 1) * rows)
        logits = (
            scale
            * jnp.dot(texts[here, :], images_turned[...], preferred_element_type=jnp.float32)
            + bias
        )
        weight = jax.nn.sigmoid(jnp.where(hit, -logits, logits)) * scale
        coef = jnp.where(hit, -weight, weight).astype(jnp.bfloat16)
        coefs[here, :] = coef
        return jnp.dot(coef, images[...], preferred_element_type=jnp.float32)

    def image_grad(which):
        return lax.dot_general(
            coefs[:, which], texts[...], (((0,), (0,)), ((), ())),
            preferred_element_type=jnp.float32,
        )

    back_a = between(A2, A2, send_a, got_a, (from_a, grp))
    back_r = between(A2, R2, send_a, got_r, (at(1), grp))
    back_b = between(B2, B2, send_b, got_b, (from_b, grp))
    back_c = between(C2, C2, send_c, got_c, (sibling, grp))
    back_x = remote(X2, X2, send_x, got_x, across)

    def pass_on(come, go):
        for i in range(CHUNKS):
            come[i].wait_recv()
            go[i].start()

    def finish_b():
        wait_recv(copy_b)
        send_b[...] = pair(AT_B, from_b).astype(jnp.bfloat16)
        start(back_b)

    def relayed_b():
        gt_b[...] = pair(AT_B, from_b)

    def relay_back():
        for i in range(CHUNKS):
            back_r[i].wait_recv()
            send_b[part(i), :] = (
                gt_b[part(i), :] + got_r[part(i), :].astype(jnp.float32)
            ).astype(jnp.bfloat16)
            back_b[i].start()

    pl.when(q == 2)(lambda: pass_on(copy_b, relay))
    pl.when(q != 1)(lambda: pass_on(copy_a, copy_c))

    copy_m.wait()
    copy_x.wait()
    images_turned[...] = images[...].T
    gt_own[...] = pair(OWN, blk)

    pl.when(odd == 1)(finish_b)
    pl.when(q == 1)(lambda: pass_on(copy_a, copy_c))

    gt_a[...] = pair(AT_A, from_a)
    wait_recv(copy_c)
    send_c[...] = pair(AT_C, from_c).astype(jnp.bfloat16)
    start(back_c)

    for i in range(CHUNKS):
        back_c[i].wait_recv()
        send_a[part(i), :] = (
            gt_a[part(i), :] + got_c[part(i), :].astype(jnp.float32)
        ).astype(jnp.bfloat16)
        pl.when(q == 1)(back_r[i].start)
        pl.when(q != 1)(back_a[i].start)

    pl.when(q == 0)(finish_b)
    pl.when(q == 2)(relayed_b)

    send_x[...] = image_grad(slice(rows, 2 * rows)).astype(jnp.bfloat16)
    back_x.start()
    pl.when(q == 2)(relay_back)
    grad = image_grad(slice(0, rows))

    back_x.wait_recv()
    grad = grad + got_x[...].astype(jnp.float32)
    out[:rows, :] = back_norm(grad, unit_i[...], inv_i[...], turned_i[...])

    def add_a():
        wait_recv(back_a)
        gt_own[...] += got_a[...].astype(jnp.float32)

    wait_recv(back_b)
    gt_own[...] += got_b[...].astype(jnp.float32)
    pl.when(q != 3)(add_a)
    out[rows:, :] = back_norm(gt_own[...], unit_t[...], inv_t[...], turned_t[...])

    pl.when(q != 3)(lambda: wait_send(copy_a))
    pl.when(q == 2)(lambda: wait_send(relay))
    for copies in (copy_b, copy_c, back_a, back_b, back_c, [back_x]):
        wait_send(copies)


def body(image_feats, text_feats, image_proj, text_proj, logit_scale, logit_bias, match):
    n = lax.axis_size("blk")
    rows, depth = image_feats.shape
    half = lambda *shape: pltpu.VMEM(shape, jnp.bfloat16)
    full = lambda *shape: pltpu.VMEM(shape, jnp.float32)
    far = pl.BlockSpec(memory_space=pltpu.HBM)
    near = pl.BlockSpec(memory_space=pltpu.VMEM)
    scalar = pl.BlockSpec(memory_space=pltpu.SMEM)
    tile = (rows, depth)
    both = pl.pallas_call(
        functools.partial(kernel, n),
        out_shape=jax.ShapeDtypeStruct((2 * rows, depth), jnp.bfloat16),
        in_specs=[far] * 4 + [scalar] * 2 + [near],
        out_specs=near,
        scratch_shapes=[
            half(*tile), half(*tile), half(depth, depth), half(depth, depth),
            half(depth, depth), half(depth, depth),
            full(*tile), full(rows, 1), full(*tile), full(rows, 1),
            half(2 * rows, depth), half(depth, 2 * rows),
            half(SPAN * rows, depth), half(SPAN * rows, 2 * rows),
            pltpu.VMEM((1, rows), jnp.int32),
            full(*tile), full(*tile), full(*tile),
            half(*tile), half(*tile), half(*tile), half(*tile),
            half(*tile), half(*tile), half(*tile), half(*tile), half(*tile),
            pltpu.SemaphoreType.DMA((4,)),
            pltpu.SemaphoreType.DMA((SEMS,)),
            pltpu.SemaphoreType.DMA((SEMS,)),
        ],
        compiler_params=pltpu.CompilerParams(
            collective_id=0, has_side_effects=True, vmem_limit_bytes=64 * 1024 * 1024
        ),
        cost_estimate=pl.CostEstimate(
            flops=8 * rows * depth * depth + 48 * rows * rows * depth,
            bytes_accessed=4 * depth * depth + 8 * rows * depth,
            transcendentals=8 * rows * rows,
        ),
    )(
        image_feats, text_feats, image_proj, text_proj, logit_scale, logit_bias,
        match.reshape(1, rows),
    )
    return both[:rows], both[rows:]


def solution(mesh):
    rows = P(("blk", "group"), None)
    return jax.shard_map(
        body,
        mesh=mesh,
        in_specs=(rows, rows, P(), P(), P(), P(), P(("blk", "group"))),
        out_specs=(rows, rows),
        check_vma=False,
    )
```

```python
import functools

import jax
import jax.numpy as jnp
from jax import lax
from jax.experimental import pallas as pl
from jax.experimental.pallas import tpu as pltpu
from jax.sharding import PartitionSpec as P

MESH = pl.DeviceIdType.MESH
SPAN = 4
OWN, AT_A, AT_C, AT_B = range(SPAN)
CHUNKS = 2
A, C, A2, C2 = range(0, 4 * CHUNKS, CHUNKS)
B, B2, X, M, X2 = range(4 * CHUNKS, 4 * CHUNKS + 5)
SEMS = 4 * CHUNKS + 5


def embed(feats, proj):
    x = jnp.dot(feats, proj, preferred_element_type=jnp.float32)
    inv = lax.rsqrt(jnp.sum(x * x, axis=-1, keepdims=True) + 1e-06)
    return x * inv, inv


def back_norm(grad, unit, inv, turned):
    inner = jnp.sum(grad * unit, axis=-1, keepdims=True)
    grad_x = (inv * (grad - inner * unit)).astype(jnp.bfloat16)
    out = jnp.dot(grad_x, turned, preferred_element_type=jnp.float32)
    return out.astype(jnp.bfloat16)


def kernel(
    n,
    image_feats, text_feats, image_proj, text_proj, matches, scale_ref, bias_ref,
    out,
    feats_i, feats_t, proj_i, proj_t, turned_i, turned_t,
    unit_i, inv_i, unit_t, inv_t, images, images_turned, texts, coefs, match, match_nbr,
    gt_own, gt_a, send_a, send_b, send_c, send_x,
    got_a, got_b, got_c, got_x,
    load_sem, send_sem, recv_sem,
):
    rows = match.shape[1]
    step = rows // CHUNKS
    blk = lax.axis_index("blk")
    grp = lax.axis_index("group")
    odd = lax.rem(blk, 2)

    def at(distance):
        return lax.rem(blk + distance + n, n)

    sibling = blk + 1 - 2 * odd
    across = (blk, 1 - grp)
    from_a, from_b, from_c = at(-2), at(2 * odd - 3), at(-1 - 2 * odd)

    loads = [
        pltpu.make_async_copy(src, dst, load_sem.at[i])
        for i, (src, dst) in enumerate(
            (
                (text_feats, feats_t),
                (text_proj, proj_t),
                (image_feats, feats_i),
                (image_proj, proj_i),
                (matches, match),
            )
        )
    ]
    loads[0].start()
    loads[1].start()
    loads[4].start()

    barrier = pltpu.get_barrier_semaphore()

    def greet(partner):
        pl.semaphore_signal(barrier, inc=1, device_id=partner, device_id_type=MESH)

    greet((sibling, grp))
    greet(across)
    greet((at(6 * odd - 3), grp))
    greet((at(2), grp))
    greet((at(-2), grp))

    def remote(role, src, dst, partner):
        return pltpu.make_async_remote_copy(
            src_ref=src, dst_ref=dst, send_sem=send_sem.at[role],
            recv_sem=recv_sem.at[role], device_id=partner, device_id_type=MESH,
        )

    def part(i):
        return pl.ds(i * step, step)

    def between(role, src, dst, partner):
        return [
            remote(role + i, src.at[part(i)], dst.at[part(i)], partner)
            for i in range(CHUNKS)
        ]

    def start(copies):
        for copy in copies:
            copy.start()

    def wait_recv(copies):
        for copy in copies:
            copy.wait_recv()

    def wait_send(copies):
        for copy in copies:
            copy.wait_send()

    def slot(place):
        return texts.at[pl.ds(place * rows, rows)]

    loads[0].wait()
    loads[1].wait()
    loads[2].start()
    loads[3].start()
    unit, inv = embed(feats_t[...], proj_t[...])
    texts[:rows, :] = unit.astype(jnp.bfloat16)

    pl.semaphore_wait(barrier, 5)
    copy_a = between(A, slot(OWN), slot(AT_A), (at(2), grp))
    copy_b = remote(B, slot(OWN), slot(AT_B), (at(1 + 2 * odd), grp))
    copy_c = between(C, slot(AT_A), slot(AT_C), (sibling, grp))
    copy_m = remote(M, match, match_nbr, across)
    start(copy_a)
    copy_b.start()
    loads[4].wait()
    copy_m.start()
    unit_t[...] = unit
    inv_t[...] = inv

    loads[2].wait()
    loads[3].wait()
    unit, inv = embed(feats_i[...], proj_i[...])
    images[:rows, :] = unit.astype(jnp.bfloat16)
    copy_x = remote(X, images.at[pl.ds(0, rows)], images.at[pl.ds(rows, rows)], across)
    copy_x.start()
    unit_i[...] = unit
    inv_i[...] = inv
    turned_t[...] = proj_t[...].T
    turned_i[...] = proj_i[...].T

    scale = scale_ref[0]
    bias = bias_ref[0]

    def pair(place, source):
        ids = (source * 2 + grp) * rows + lax.broadcasted_iota(
            jnp.int32, (rows, 2 * rows), 0
        )
        wanted = jnp.concatenate([match[...], match_nbr[...]], axis=1)
        hit = wanted == ids
        here = slice(place * rows, (place + 1) * rows)
        logits = (
            scale
            * jnp.dot(texts[here, :], images_turned[...], preferred_element_type=jnp.float32)
            + bias
        )
        weight = jax.nn.sigmoid(jnp.where(hit, -logits, logits)) * scale
        coef = jnp.where(hit, -weight, weight).astype(jnp.bfloat16)
        coefs[here, :] = coef
        return jnp.dot(coef, images[...], preferred_element_type=jnp.float32)

    def image_grad(which):
        return lax.dot_general(
            coefs[:, which], texts[...], (((0,), (0,)), ((), ())),
            preferred_element_type=jnp.float32,
        )

    back_a = between(A2, send_a, got_a, (from_a, grp))
    back_b = remote(B2, send_b, got_b, (from_b, grp))
    back_c = between(C2, send_c, got_c, (sibling, grp))
    back_x = remote(X2, send_x, got_x, across)

    def pass_on(come, go):
        for i in range(CHUNKS):
            come[i].wait_recv()
            go[i].start()

    def finish_b():
        copy_b.wait_recv()
        send_b[...] = pair(AT_B, from_b).astype(jnp.bfloat16)
        back_b.start()

    pass_on(copy_a, copy_c)
    copy_m.wait()
    copy_x.wait()
    images_turned[...] = images[...].T
    gt_own[...] = pair(OWN, blk)

    pl.when(odd == 1)(finish_b)

    gt_a[...] = pair(AT_A, from_a)
    wait_recv(copy_c)
    send_c[...] = pair(AT_C, from_c).astype(jnp.bfloat16)
    start(back_c)

    for i in range(CHUNKS):
        back_c[i].wait_recv()
        send_a[part(i), :] = (
            gt_a[part(i), :] + got_c[part(i), :].astype(jnp.float32)
        ).astype(jnp.bfloat16)
        back_a[i].start()

    pl.when(odd == 0)(finish_b)

    send_x[...] = image_grad(slice(rows, 2 * rows)).astype(jnp.bfloat16)
    back_x.start()
    grad = image_grad(slice(0, rows))

    back_x.wait_recv()
    grad = grad + got_x[...].astype(jnp.float32)
    out[:rows, :] = back_norm(grad, unit_i[...], inv_i[...], turned_i[...])

    back_b.wait_recv()
    gt_own[...] += got_b[...].astype(jnp.float32)
    wait_recv(back_a)
    grad = gt_own[...] + got_a[...].astype(jnp.float32)
    out[rows:, :] = back_norm(grad, unit_t[...], inv_t[...], turned_t[...])

    for copies in (copy_a, [copy_b], copy_c, back_a, [back_b], back_c, [back_x]):
        wait_send(copies)


def body(image_feats, text_feats, image_proj, text_proj, logit_scale, logit_bias, match):
    n = lax.axis_size("blk")
    rows, depth = image_feats.shape
    half = lambda *shape: pltpu.VMEM(shape, jnp.bfloat16)
    full = lambda *shape: pltpu.VMEM(shape, jnp.float32)
    far = pl.BlockSpec(memory_space=pltpu.HBM)
    near = pl.BlockSpec(memory_space=pltpu.VMEM)
    scalar = pl.BlockSpec(memory_space=pltpu.SMEM)
    tile = (rows, depth)
    both = pl.pallas_call(
        functools.partial(kernel, n),
        out_shape=jax.ShapeDtypeStruct((2 * rows, depth), jnp.bfloat16),
        in_specs=[far] * 5 + [scalar] * 2,
        out_specs=near,
        scratch_shapes=[
            half(*tile), half(*tile), half(depth, depth), half(depth, depth),
            half(depth, depth), half(depth, depth),
            full(*tile), full(rows, 1), full(*tile), full(rows, 1),
            half(2 * rows, depth), half(depth, 2 * rows),
            half(SPAN * rows, depth), half(SPAN * rows, 2 * rows),
            pltpu.VMEM((1, rows), jnp.int32), pltpu.VMEM((1, rows), jnp.int32),
            full(*tile), full(*tile),
            half(*tile), half(*tile), half(*tile), half(*tile),
            half(*tile), half(*tile), half(*tile), half(*tile),
            pltpu.SemaphoreType.DMA((5,)),
            pltpu.SemaphoreType.DMA((SEMS,)),
            pltpu.SemaphoreType.DMA((SEMS,)),
        ],
        compiler_params=pltpu.CompilerParams(
            collective_id=0, has_side_effects=True, vmem_limit_bytes=32 * 1024 * 1024
        ),
        cost_estimate=pl.CostEstimate(
            flops=8 * rows * depth * depth + 48 * rows * rows * depth,
            bytes_accessed=4 * depth * depth + 8 * rows * depth,
            transcendentals=8 * rows * rows,
        ),
    )(
        *(
            pltpu.with_memory_space_constraint(x, pltpu.HBM)
            for x in (image_feats, text_feats, image_proj, text_proj, match.reshape(1, rows))
        ),
        logit_scale, logit_bias,
    )
    return both[:rows], both[rows:]


def solution(mesh):
    rows = P(("blk", "group"), None)
    return jax.shard_map(
        body,
        mesh=mesh,
        in_specs=(rows, rows, P(), P(), P(), P(), P(("blk", "group"))),
        out_specs=(rows, rows),
        check_vma=False,
    )
```

```python
import functools

import jax
import jax.numpy as jnp
from jax import lax
from jax.experimental import pallas as pl
from jax.experimental.pallas import tpu as pltpu
from jax.sharding import PartitionSpec as P

MESH = pl.DeviceIdType.MESH
SPAN = 4
OWN, AT_A, AT_C, AT_B = range(SPAN)
CHUNKS = 2
PARTS = 3
A, C, A2, C2 = range(0, 4 * CHUNKS, CHUNKS)
B, B2, X, M, X2 = range(4 * CHUNKS, 4 * CHUNKS + 5)
SEMS = 4 * CHUNKS + 5


def embed(feats, proj, loads):
    part = proj.shape[0] // PARTS
    x = 0.0
    for i, load in enumerate(loads):
        load.wait()
        here = slice(i * part, (i + 1) * part)
        x = x + jnp.dot(feats[:, here], proj[here, :], preferred_element_type=jnp.float32)
    inv = lax.rsqrt(jnp.sum(x * x, axis=-1, keepdims=True) + 1e-06)
    return x * inv, inv


def back_norm(grad, unit, inv, turned):
    inner = jnp.sum(grad * unit, axis=-1, keepdims=True)
    grad_x = (inv * (grad - inner * unit)).astype(jnp.bfloat16)
    out = jnp.dot(grad_x, turned, preferred_element_type=jnp.float32)
    return out.astype(jnp.bfloat16)


def kernel(
    n,
    image_feats, text_feats, image_proj, text_proj, matches, scale_ref, bias_ref,
    out,
    feats_i, feats_t, proj_i, proj_t, turned_i, turned_t,
    unit_i, inv_i, unit_t, inv_t, images, images_turned, texts, coefs, match, match_nbr,
    gt_own, gt_a, send_a, send_b, send_c, send_x,
    got_a, got_b, got_c, got_x,
    load_sem, send_sem, recv_sem,
):
    rows = match.shape[1]
    step = rows // CHUNKS
    blk = lax.axis_index("blk")
    grp = lax.axis_index("group")
    odd = lax.rem(blk, 2)

    def at(distance):
        return lax.rem(blk + distance + n, n)

    sibling = blk + 1 - 2 * odd
    across = (blk, 1 - grp)
    from_a, from_b, from_c = at(-2), at(2 * odd - 3), at(-1 - 2 * odd)

    def load(src, dst, sem):
        return pltpu.make_async_copy(src, dst, load_sem.at[sem])

    def load_parts(src, dst, sem):
        part = src.shape[0] // PARTS
        return [
            load(src.at[pl.ds(i * part, part)], dst.at[pl.ds(i * part, part)], sem + i)
            for i in range(PARTS)
        ]

    def start(copies):
        for copy in copies:
            copy.start()

    load_t = load(text_feats, feats_t, 0)
    load_i = load(image_feats, feats_i, 1)
    load_m = load(matches, match, 2)
    loads_t = load_parts(text_proj, proj_t, 3)
    loads_i = load_parts(image_proj, proj_i, 3 + PARTS)
    load_t.start()
    start(loads_t)
    load_i.start()
    start(loads_i)
    load_m.start()

    barrier = pltpu.get_barrier_semaphore()

    def greet(partner):
        pl.semaphore_signal(barrier, inc=1, device_id=partner, device_id_type=MESH)

    greet((sibling, grp))
    greet(across)
    greet((at(6 * odd - 3), grp))
    greet((at(2), grp))
    greet((at(-2), grp))

    def remote(role, src, dst, partner):
        return pltpu.make_async_remote_copy(
            src_ref=src, dst_ref=dst, send_sem=send_sem.at[role],
            recv_sem=recv_sem.at[role], device_id=partner, device_id_type=MESH,
        )

    def part(i):
        return pl.ds(i * step, step)

    def between(role, src, dst, partner):
        return [
            remote(role + i, src.at[part(i)], dst.at[part(i)], partner)
            for i in range(CHUNKS)
        ]

    def wait_recv(copies):
        for copy in copies:
            copy.wait_recv()

    def wait_send(copies):
        for copy in copies:
            copy.wait_send()

    def slot(place):
        return texts.at[pl.ds(place * rows, rows)]

    load_t.wait()
    unit, inv = embed(feats_t, proj_t, loads_t)
    texts[:rows, :] = unit.astype(jnp.bfloat16)

    pl.semaphore_wait(barrier, 5)
    copy_a = between(A, slot(OWN), slot(AT_A), (at(2), grp))
    copy_b = remote(B, slot(OWN), slot(AT_B), (at(1 + 2 * odd), grp))
    copy_c = between(C, slot(AT_A), slot(AT_C), (sibling, grp))
    copy_m = remote(M, match, match_nbr, across)
    start(copy_a)
    copy_b.start()
    load_m.wait()
    copy_m.start()
    unit_t[...] = unit
    inv_t[...] = inv

    load_i.wait()
    unit, inv = embed(feats_i, proj_i, loads_i)
    images[:rows, :] = unit.astype(jnp.bfloat16)
    copy_x = remote(X, images.at[pl.ds(0, rows)], images.at[pl.ds(rows, rows)], across)
    copy_x.start()
    unit_i[...] = unit
    inv_i[...] = inv

    scale = scale_ref[0]
    bias = bias_ref[0]

    def pair(place, source):
        ids = (source * 2 + grp) * rows + lax.broadcasted_iota(
            jnp.int32, (rows, 2 * rows), 0
        )
        wanted = jnp.concatenate([match[...], match_nbr[...]], axis=1)
        hit = wanted == ids
        here = slice(place * rows, (place + 1) * rows)
        logits = (
            scale
            * jnp.dot(texts[here, :], images_turned[...], preferred_element_type=jnp.float32)
            + bias
        )
        weight = jax.nn.sigmoid(jnp.where(hit, -logits, logits)) * scale
        coef = jnp.where(hit, -weight, weight).astype(jnp.bfloat16)
        coefs[here, :] = coef
        return jnp.dot(coef, images[...], preferred_element_type=jnp.float32)

    def image_grad(which):
        return lax.dot_general(
            coefs[:, which], texts[...], (((0,), (0,)), ((), ())),
            preferred_element_type=jnp.float32,
        )

    back_a = between(A2, send_a, got_a, (from_a, grp))
    back_b = remote(B2, send_b, got_b, (from_b, grp))
    back_c = between(C2, send_c, got_c, (sibling, grp))
    back_x = remote(X2, send_x, got_x, across)

    def pass_on(come, go):
        for i in range(CHUNKS):
            come[i].wait_recv()
            go[i].start()

    def finish_b():
        copy_b.wait_recv()
        send_b[...] = pair(AT_B, from_b).astype(jnp.bfloat16)
        back_b.start()

    pass_on(copy_a, copy_c)
    copy_m.wait()
    copy_x.wait()
    images_turned[...] = images[...].T
    pl.when(odd == 1)(finish_b)
    gt_a[...] = pair(AT_A, from_a)
    gt_own[...] = pair(OWN, blk)

    wait_recv(copy_c)
    send_c[...] = pair(AT_C, from_c).astype(jnp.bfloat16)
    start(back_c)
    pl.when(odd == 0)(finish_b)

    for i in range(CHUNKS):
        back_c[i].wait_recv()
        send_a[part(i), :] = (
            gt_a[part(i), :] + got_c[part(i), :].astype(jnp.float32)
        ).astype(jnp.bfloat16)
        back_a[i].start()

    send_x[...] = image_grad(slice(rows, 2 * rows)).astype(jnp.bfloat16)
    back_x.start()
    turned_i[...] = proj_i[...].T
    turned_t[...] = proj_t[...].T
    grad = image_grad(slice(0, rows))

    back_x.wait_recv()
    grad = grad + got_x[...].astype(jnp.float32)
    out[:rows, :] = back_norm(grad, unit_i[...], inv_i[...], turned_i[...])

    back_b.wait_recv()
    gt_own[...] += got_b[...].astype(jnp.float32)
    wait_recv(back_a)
    grad = gt_own[...] + got_a[...].astype(jnp.float32)
    out[rows:, :] = back_norm(grad, unit_t[...], inv_t[...], turned_t[...])

    for copies in (copy_a, [copy_b], copy_c, back_a, [back_b], back_c, [back_x]):
        wait_send(copies)


def body(image_feats, text_feats, image_proj, text_proj, logit_scale, logit_bias, match):
    n = lax.axis_size("blk")
    rows, depth = image_feats.shape
    half = lambda *shape: pltpu.VMEM(shape, jnp.bfloat16)
    full = lambda *shape: pltpu.VMEM(shape, jnp.float32)
    far = pl.BlockSpec(memory_space=pltpu.HBM)
    near = pl.BlockSpec(memory_space=pltpu.VMEM)
    scalar = pl.BlockSpec(memory_space=pltpu.SMEM)
    tile = (rows, depth)
    both = pl.pallas_call(
        functools.partial(kernel, n),
        out_shape=jax.ShapeDtypeStruct((2 * rows, depth), jnp.bfloat16),
        in_specs=[far] * 5 + [scalar] * 2,
        out_specs=near,
        scratch_shapes=[
            half(*tile), half(*tile), half(depth, depth), half(depth, depth),
            half(depth, depth), half(depth, depth),
            full(*tile), full(rows, 1), full(*tile), full(rows, 1),
            half(2 * rows, depth), half(depth, 2 * rows),
            half(SPAN * rows, depth), half(SPAN * rows, 2 * rows),
            pltpu.VMEM((1, rows), jnp.int32), pltpu.VMEM((1, rows), jnp.int32),
            full(*tile), full(*tile),
            half(*tile), half(*tile), half(*tile), half(*tile),
            half(*tile), half(*tile), half(*tile), half(*tile),
            pltpu.SemaphoreType.DMA((3 + 2 * PARTS,)),
            pltpu.SemaphoreType.DMA((SEMS,)),
            pltpu.SemaphoreType.DMA((SEMS,)),
        ],
        compiler_params=pltpu.CompilerParams(
            collective_id=0, has_side_effects=True, vmem_limit_bytes=32 * 1024 * 1024
        ),
        cost_estimate=pl.CostEstimate(
            flops=8 * rows * depth * depth + 48 * rows * rows * depth,
            bytes_accessed=4 * depth * depth + 8 * rows * depth,
            transcendentals=8 * rows * rows,
        ),
    )(
        *(
            pltpu.with_memory_space_constraint(x, pltpu.HBM)
            for x in (image_feats, text_feats, image_proj, text_proj, match.reshape(1, rows))
        ),
        logit_scale, logit_bias,
    )
    return both[:rows], both[rows:]


def solution(mesh):
    rows = P(("blk", "group"), None)
    return jax.shard_map(
        body,
        mesh=mesh,
        in_specs=(rows, rows, P(), P(), P(), P(), P(("blk", "group"))),
        out_specs=(rows, rows),
        check_vma=False,
    )
```

```python
import functools

import jax
import jax.numpy as jnp
from jax import lax
from jax.experimental import pallas as pl
from jax.experimental.pallas import tpu as pltpu
from jax.sharding import PartitionSpec as P

MESH = pl.DeviceIdType.MESH
SPAN = 4
OWN, AT_A, AT_C, AT_B = range(SPAN)
CHUNKS = 2
PARTS = 3
A, C, A2, C2 = range(0, 4 * CHUNKS, CHUNKS)
B, B2, X, M, X2 = range(4 * CHUNKS, 4 * CHUNKS + 5)
SEMS = 4 * CHUNKS + 5


def embed(feats, proj, loads):
    part = proj.shape[0] // PARTS
    x = 0.0
    for i, load in enumerate(loads):
        load.wait()
        here = slice(i * part, (i + 1) * part)
        x = x + jnp.dot(feats[:, here], proj[here, :], preferred_element_type=jnp.float32)
    inv = lax.rsqrt(jnp.sum(x * x, axis=-1, keepdims=True) + 1e-06)
    return x * inv, inv


def back_norm(grad, unit, inv, turned):
    inner = jnp.sum(grad * unit, axis=-1, keepdims=True)
    grad_x = (inv * (grad - inner * unit)).astype(jnp.bfloat16)
    out = jnp.dot(grad_x, turned, preferred_element_type=jnp.float32)
    return out.astype(jnp.bfloat16)


def kernel(
    n,
    image_feats, text_feats, image_proj, text_proj, matches, scale_ref, bias_ref,
    out,
    feats_i, feats_t, proj_i, proj_t, turned_i, turned_t,
    unit_i, inv_i, unit_t, inv_t, images, images_turned, texts, coefs, match, match_nbr,
    gi_own, gt_own, gt_a, send_a, send_b, send_c, send_x,
    got_a, got_b, got_c, got_x,
    load_sem, send_sem, recv_sem,
):
    rows = match.shape[1]
    step = rows // CHUNKS
    blk = lax.axis_index("blk")
    grp = lax.axis_index("group")
    odd = lax.rem(blk, 2)

    def at(distance):
        return lax.rem(blk + distance + n, n)

    sibling = blk + 1 - 2 * odd
    across = (blk, 1 - grp)
    from_a, from_b, from_c = at(-2), at(2 * odd - 3), at(-1 - 2 * odd)

    def load(src, dst, sem):
        return pltpu.make_async_copy(src, dst, load_sem.at[sem])

    def load_parts(src, dst, sem):
        part = src.shape[0] // PARTS
        return [
            load(src.at[pl.ds(i * part, part)], dst.at[pl.ds(i * part, part)], sem + i)
            for i in range(PARTS)
        ]

    def start(copies):
        for copy in copies:
            copy.start()

    load_t = load(text_feats, feats_t, 0)
    load_i = load(image_feats, feats_i, 1)
    load_m = load(matches, match, 2)
    loads_t = load_parts(text_proj, proj_t, 3)
    loads_i = load_parts(image_proj, proj_i, 3 + PARTS)
    load_t.start()
    start(loads_t)
    load_i.start()
    start(loads_i)
    load_m.start()

    barrier = pltpu.get_barrier_semaphore()

    def greet(partner):
        pl.semaphore_signal(barrier, inc=1, device_id=partner, device_id_type=MESH)

    greet((sibling, grp))
    greet(across)
    greet((at(6 * odd - 3), grp))
    greet((at(2), grp))
    greet((at(-2), grp))

    def remote(role, src, dst, partner):
        return pltpu.make_async_remote_copy(
            src_ref=src, dst_ref=dst, send_sem=send_sem.at[role],
            recv_sem=recv_sem.at[role], device_id=partner, device_id_type=MESH,
        )

    def part(i):
        return pl.ds(i * step, step)

    def between(role, src, dst, partner):
        return [
            remote(role + i, src.at[part(i)], dst.at[part(i)], partner)
            for i in range(CHUNKS)
        ]

    def wait_recv(copies):
        for copy in copies:
            copy.wait_recv()

    def wait_send(copies):
        for copy in copies:
            copy.wait_send()

    def slot(place):
        return texts.at[pl.ds(place * rows, rows)]

    load_t.wait()
    unit, inv = embed(feats_t, proj_t, loads_t)
    texts[:rows, :] = unit.astype(jnp.bfloat16)

    pl.semaphore_wait(barrier, 5)
    copy_a = between(A, slot(OWN), slot(AT_A), (at(2), grp))
    copy_b = remote(B, slot(OWN), slot(AT_B), (at(1 + 2 * odd), grp))
    copy_c = between(C, slot(AT_A), slot(AT_C), (sibling, grp))
    copy_m = remote(M, match, match_nbr, across)
    start(copy_a)
    pl.when(odd == 0)(copy_b.start)
    load_m.wait()
    copy_m.start()
    unit_t[...] = unit
    inv_t[...] = inv

    load_i.wait()
    unit, inv = embed(feats_i, proj_i, loads_i)
    images[:rows, :] = unit.astype(jnp.bfloat16)
    copy_x = remote(X, images.at[pl.ds(0, rows)], images.at[pl.ds(rows, rows)], across)
    copy_x.start()
    unit_i[...] = unit
    inv_i[...] = inv

    scale = scale_ref[0]
    bias = bias_ref[0]

    def pair(place, source):
        ids = (source * 2 + grp) * rows + lax.broadcasted_iota(
            jnp.int32, (rows, 2 * rows), 0
        )
        wanted = jnp.concatenate([match[...], match_nbr[...]], axis=1)
        hit = wanted == ids
        here = slice(place * rows, (place + 1) * rows)
        logits = (
            scale
            * jnp.dot(texts[here, :], images_turned[...], preferred_element_type=jnp.float32)
            + bias
        )
        weight = jax.nn.sigmoid(jnp.where(hit, -logits, logits)) * scale
        coef = jnp.where(hit, -weight, weight).astype(jnp.bfloat16)
        coefs[here, :] = coef
        return jnp.dot(coef, images[...], preferred_element_type=jnp.float32)

    def image_grad(which):
        return lax.dot_general(
            coefs[:, which], texts[...], (((0,), (0,)), ((), ())),
            preferred_element_type=jnp.float32,
        )

    back_a = between(A2, send_a, got_a, (from_a, grp))
    back_b = remote(B2, send_b, got_b, (from_b, grp))
    back_c = between(C2, send_c, got_c, (sibling, grp))
    back_x = remote(X2, send_x, got_x, across)

    def pass_on(come, go):
        for i in range(CHUNKS):
            come[i].wait_recv()
            go[i].start()

    def finish_b():
        copy_b.wait_recv()
        send_b[...] = pair(AT_B, from_b).astype(jnp.bfloat16)
        back_b.start()

    def late_b():
        wait_send(copy_a)
        copy_b.start()

    pl.when(odd == 1)(late_b)
    pass_on(copy_a, copy_c)
    copy_m.wait()
    copy_x.wait()
    images_turned[...] = images[...].T
    pl.when(odd == 1)(finish_b)
    gt_a[...] = pair(AT_A, from_a)
    gt_own[...] = pair(OWN, blk)

    wait_recv(copy_c)
    send_c[...] = pair(AT_C, from_c).astype(jnp.bfloat16)
    start(back_c)
    pl.when(odd == 0)(finish_b)

    for i in range(CHUNKS):
        back_c[i].wait_recv()
        send_a[part(i), :] = (
            gt_a[part(i), :] + got_c[part(i), :].astype(jnp.float32)
        ).astype(jnp.bfloat16)
        back_a[i].start()

    send_x[...] = image_grad(slice(rows, 2 * rows)).astype(jnp.bfloat16)
    back_x.start()
    turned_i[...] = proj_i[...].T
    turned_t[...] = proj_t[...].T
    gi_own[...] = image_grad(slice(0, rows))

    def finish_image():
        back_x.wait_recv()
        grad = gi_own[...] + got_x[...].astype(jnp.float32)
        out[:rows, :] = back_norm(grad, unit_i[...], inv_i[...], turned_i[...])

    def finish_text():
        back_b.wait_recv()
        gt_own[...] += got_b[...].astype(jnp.float32)
        wait_recv(back_a)
        grad = gt_own[...] + got_a[...].astype(jnp.float32)
        out[rows:, :] = back_norm(grad, unit_t[...], inv_t[...], turned_t[...])

    pl.when(blk < 2)(finish_text)
    finish_image()
    pl.when(blk >= 2)(finish_text)

    pl.when(odd == 0)(lambda: wait_send(copy_a))
    for copies in ([copy_b], copy_c, back_a, [back_b], back_c, [back_x]):
        wait_send(copies)


def body(image_feats, text_feats, image_proj, text_proj, logit_scale, logit_bias, match):
    n = lax.axis_size("blk")
    rows, depth = image_feats.shape
    half = lambda *shape: pltpu.VMEM(shape, jnp.bfloat16)
    full = lambda *shape: pltpu.VMEM(shape, jnp.float32)
    far = pl.BlockSpec(memory_space=pltpu.HBM)
    near = pl.BlockSpec(memory_space=pltpu.VMEM)
    scalar = pl.BlockSpec(memory_space=pltpu.SMEM)
    tile = (rows, depth)
    both = pl.pallas_call(
        functools.partial(kernel, n),
        out_shape=jax.ShapeDtypeStruct((2 * rows, depth), jnp.bfloat16),
        in_specs=[far] * 5 + [scalar] * 2,
        out_specs=near,
        scratch_shapes=[
            half(*tile), half(*tile), half(depth, depth), half(depth, depth),
            half(depth, depth), half(depth, depth),
            full(*tile), full(rows, 1), full(*tile), full(rows, 1),
            half(2 * rows, depth), half(depth, 2 * rows),
            half(SPAN * rows, depth), half(SPAN * rows, 2 * rows),
            pltpu.VMEM((1, rows), jnp.int32), pltpu.VMEM((1, rows), jnp.int32),
            full(*tile), full(*tile), full(*tile),
            half(*tile), half(*tile), half(*tile), half(*tile),
            half(*tile), half(*tile), half(*tile), half(*tile),
            pltpu.SemaphoreType.DMA((3 + 2 * PARTS,)),
            pltpu.SemaphoreType.DMA((SEMS,)),
            pltpu.SemaphoreType.DMA((SEMS,)),
        ],
        compiler_params=pltpu.CompilerParams(
            collective_id=0, has_side_effects=True, vmem_limit_bytes=32 * 1024 * 1024
        ),
        cost_estimate=pl.CostEstimate(
            flops=8 * rows * depth * depth + 48 * rows * rows * depth,
            bytes_accessed=4 * depth * depth + 8 * rows * depth,
            transcendentals=8 * rows * rows,
        ),
    )(
        *(
            pltpu.with_memory_space_constraint(x, pltpu.HBM)
            for x in (image_feats, text_feats, image_proj, text_proj, match.reshape(1, rows))
        ),
        logit_scale, logit_bias,
    )
    return both[:rows], both[rows:]


def solution(mesh):
    rows = P(("blk", "group"), None)
    return jax.shard_map(
        body,
        mesh=mesh,
        in_specs=(rows, rows, P(), P(), P(), P(), P(("blk", "group"))),
        out_specs=(rows, rows),
        check_vma=False,
    )
```

```python
import functools

import jax
import jax.numpy as jnp
from jax import lax
from jax.experimental import pallas as pl
from jax.experimental.pallas import tpu as pltpu
from jax.sharding import PartitionSpec as P

MESH = pl.DeviceIdType.MESH
SPAN = 4
OWN, AT_A, AT_C, AT_B = range(SPAN)
CHUNKS = 2
PARTS = 3
A, C, A2, C2 = range(0, 4 * CHUNKS, CHUNKS)
B, B2, X, M, X2 = range(4 * CHUNKS, 4 * CHUNKS + 5)
SEMS = 4 * CHUNKS + 5


def embed(feats, proj, loads):
    part = proj.shape[0] // PARTS
    x = 0.0
    for i, load in enumerate(loads):
        load.wait()
        here = slice(i * part, (i + 1) * part)
        x = x + jnp.dot(feats[:, here], proj[here, :], preferred_element_type=jnp.float32)
    inv = lax.rsqrt(jnp.sum(x * x, axis=-1, keepdims=True) + 1e-06)
    return x * inv, inv


def back_norm(grad, unit, inv, turned):
    inner = jnp.sum(grad * unit, axis=-1, keepdims=True)
    grad_x = (inv * (grad - inner * unit)).astype(jnp.bfloat16)
    out = jnp.dot(grad_x, turned, preferred_element_type=jnp.float32)
    return out.astype(jnp.bfloat16)


def kernel(
    n,
    image_feats, text_feats, image_proj, text_proj, matches, scale_ref, bias_ref,
    out,
    feats_i, feats_t, proj_i, proj_t, turned_i, turned_t,
    unit_i, inv_i, unit_t, inv_t, images, images_turned, texts, coefs, match, match_nbr,
    gi, gt_own, gt_a, send_a, send_b, send_c, send_x,
    got_a, got_b, got_c, got_x,
    load_sem, send_sem, recv_sem,
):
    rows = match.shape[1]
    step = rows // CHUNKS
    blk = lax.axis_index("blk")
    grp = lax.axis_index("group")
    odd = lax.rem(blk, 2)
    q = lax.rem(blk, 4)

    def at(distance):
        return lax.rem(blk + distance + n, n)

    sibling = blk + 1 - 2 * odd
    across = (blk, 1 - grp)
    from_a, from_b, from_c = at(-2), at(2 * odd - 3), at(-1 - 2 * odd)

    def load(src, dst, sem):
        return pltpu.make_async_copy(src, dst, load_sem.at[sem])

    def load_parts(src, dst, sem):
        part = src.shape[0] // PARTS
        return [
            load(src.at[pl.ds(i * part, part)], dst.at[pl.ds(i * part, part)], sem + i)
            for i in range(PARTS)
        ]

    def start(copies):
        for copy in copies:
            copy.start()

    load_t = load(text_feats, feats_t, 0)
    load_i = load(image_feats, feats_i, 1)
    load_m = load(matches, match, 2)
    loads_t = load_parts(text_proj, proj_t, 3)
    loads_i = load_parts(image_proj, proj_i, 3 + PARTS)
    load_t.start()
    start(loads_t)
    load_i.start()
    start(loads_i)
    load_m.start()

    barrier = pltpu.get_barrier_semaphore()

    def greet(partner):
        pl.semaphore_signal(barrier, inc=1, device_id=partner, device_id_type=MESH)

    greet((sibling, grp))
    greet(across)
    greet((at(6 * odd - 3), grp))
    greet((at(2), grp))
    greet((at(-2), grp))

    def remote(role, src, dst, partner):
        return pltpu.make_async_remote_copy(
            src_ref=src, dst_ref=dst, send_sem=send_sem.at[role],
            recv_sem=recv_sem.at[role], device_id=partner, device_id_type=MESH,
        )

    def part(i):
        return pl.ds(i * step, step)

    def between(role, src, dst, partner):
        return [
            remote(role + i, src.at[part(i)], dst.at[part(i)], partner)
            for i in range(CHUNKS)
        ]

    def wait_recv(copies):
        for copy in copies:
            copy.wait_recv()

    def wait_send(copies):
        for copy in copies:
            copy.wait_send()

    def slot(place):
        return texts.at[pl.ds(place * rows, rows)]

    load_t.wait()
    unit, inv = embed(feats_t, proj_t, loads_t)
    texts[:rows, :] = unit.astype(jnp.bfloat16)

    pl.semaphore_wait(barrier, 5)
    copy_a = between(A, slot(OWN), slot(AT_A), (at(2), grp))
    copy_b = remote(B, slot(OWN), slot(AT_B), (at(1 + 2 * odd), grp))
    copy_c = between(C, slot(AT_A), slot(AT_C), (sibling, grp))
    copy_m = remote(M, match, match_nbr, across)
    start(copy_a)
    pl.when(odd == 0)(copy_b.start)
    load_m.wait()
    copy_m.start()
    unit_t[...] = unit
    inv_t[...] = inv

    load_i.wait()
    unit, inv = embed(feats_i, proj_i, loads_i)
    images[:rows, :] = unit.astype(jnp.bfloat16)
    copy_x = remote(X, images.at[pl.ds(0, rows)], images.at[pl.ds(rows, rows)], across)
    copy_x.start()
    unit_i[...] = unit
    inv_i[...] = inv

    scale = scale_ref[0]
    bias = bias_ref[0]

    def pair(place, source):
        ids = (source * 2 + grp) * rows + lax.broadcasted_iota(
            jnp.int32, (rows, 2 * rows), 0
        )
        wanted = jnp.concatenate([match[...], match_nbr[...]], axis=1)
        hit = wanted == ids
        here = slice(place * rows, (place + 1) * rows)
        logits = (
            scale
            * jnp.dot(texts[here, :], images_turned[...], preferred_element_type=jnp.float32)
            + bias
        )
        weight = jax.nn.sigmoid(jnp.where(hit, -logits, logits)) * scale
        coef = jnp.where(hit, -weight, weight).astype(jnp.bfloat16)
        coefs[here, :] = coef
        return jnp.dot(coef, images[...], preferred_element_type=jnp.float32)

    def image_grad(here):
        return lax.dot_general(
            coefs[here, :], texts[here, :], (((0,), (0,)), ((), ())),
            preferred_element_type=jnp.float32,
        )

    back_a = between(A2, send_a, got_a, (from_a, grp))
    back_b = remote(B2, send_b, got_b, (from_b, grp))
    back_c = between(C2, send_c, got_c, (sibling, grp))
    back_x = remote(X2, send_x, got_x, across)

    def pass_on(come, go):
        for i in range(CHUNKS):
            come[i].wait_recv()
            go[i].start()

    def finish_b():
        copy_b.wait_recv()
        send_b[...] = pair(AT_B, from_b).astype(jnp.bfloat16)
        back_b.start()

    def late_b():
        wait_send(copy_a)
        copy_b.start()

    pl.when(odd == 1)(late_b)
    pass_on(copy_a, copy_c)
    copy_m.wait()
    copy_x.wait()
    images_turned[...] = images[...].T
    pl.when(odd == 1)(finish_b)
    gt_a[...] = pair(AT_A, from_a)
    gt_own[...] = pair(OWN, blk)

    wait_recv(copy_c)
    send_c[...] = pair(AT_C, from_c).astype(jnp.bfloat16)
    start(back_c)
    gi[...] = image_grad(slice(0, AT_B * rows))
    pl.when(q == 2)(finish_b)

    for i in range(CHUNKS):
        back_c[i].wait_recv()
        send_a[part(i), :] = (
            gt_a[part(i), :] + got_c[part(i), :].astype(jnp.float32)
        ).astype(jnp.bfloat16)
        back_a[i].start()

    pl.when(q == 0)(finish_b)

    gi[...] += image_grad(slice(AT_B * rows, SPAN * rows))
    send_x[...] = gi[rows:, :].astype(jnp.bfloat16)
    back_x.start()
    turned_i[...] = proj_i[...].T
    turned_t[...] = proj_t[...].T

    def finish_image():
        back_x.wait_recv()
        grad = gi[:rows, :] + got_x[...].astype(jnp.float32)
        out[:rows, :] = back_norm(grad, unit_i[...], inv_i[...], turned_i[...])

    def finish_text():
        back_b.wait_recv()
        gt_own[...] += got_b[...].astype(jnp.float32)
        wait_recv(back_a)
        grad = gt_own[...] + got_a[...].astype(jnp.float32)
        out[rows:, :] = back_norm(grad, unit_t[...], inv_t[...], turned_t[...])

    pl.when(blk < 2)(finish_text)
    finish_image()
    pl.when(blk >= 2)(finish_text)

    pl.when(odd == 0)(lambda: wait_send(copy_a))
    for copies in ([copy_b], copy_c, back_a, [back_b], back_c, [back_x]):
        wait_send(copies)


def body(image_feats, text_feats, image_proj, text_proj, logit_scale, logit_bias, match):
    n = lax.axis_size("blk")
    rows, depth = image_feats.shape
    half = lambda *shape: pltpu.VMEM(shape, jnp.bfloat16)
    full = lambda *shape: pltpu.VMEM(shape, jnp.float32)
    far = pl.BlockSpec(memory_space=pltpu.HBM)
    near = pl.BlockSpec(memory_space=pltpu.VMEM)
    scalar = pl.BlockSpec(memory_space=pltpu.SMEM)
    tile = (rows, depth)
    both = pl.pallas_call(
        functools.partial(kernel, n),
        out_shape=jax.ShapeDtypeStruct((2 * rows, depth), jnp.bfloat16),
        in_specs=[far] * 5 + [scalar] * 2,
        out_specs=near,
        scratch_shapes=[
            half(*tile), half(*tile), half(depth, depth), half(depth, depth),
            half(depth, depth), half(depth, depth),
            full(*tile), full(rows, 1), full(*tile), full(rows, 1),
            half(2 * rows, depth), half(depth, 2 * rows),
            half(SPAN * rows, depth), half(SPAN * rows, 2 * rows),
            pltpu.VMEM((1, rows), jnp.int32), pltpu.VMEM((1, rows), jnp.int32),
            full(2 * rows, depth), full(*tile), full(*tile),
            half(*tile), half(*tile), half(*tile), half(*tile),
            half(*tile), half(*tile), half(*tile), half(*tile),
            pltpu.SemaphoreType.DMA((3 + 2 * PARTS,)),
            pltpu.SemaphoreType.DMA((SEMS,)),
            pltpu.SemaphoreType.DMA((SEMS,)),
        ],
        compiler_params=pltpu.CompilerParams(
            collective_id=0, has_side_effects=True, vmem_limit_bytes=32 * 1024 * 1024
        ),
        cost_estimate=pl.CostEstimate(
            flops=8 * rows * depth * depth + 48 * rows * rows * depth,
            bytes_accessed=4 * depth * depth + 8 * rows * depth,
            transcendentals=8 * rows * rows,
        ),
    )(
        *(
            pltpu.with_memory_space_constraint(x, pltpu.HBM)
            for x in (image_feats, text_feats, image_proj, text_proj, match.reshape(1, rows))
        ),
        logit_scale, logit_bias,
    )
    return both[:rows], both[rows:]


def solution(mesh):
    rows = P(("blk", "group"), None)
    return jax.shard_map(
        body,
        mesh=mesh,
        in_specs=(rows, rows, P(), P(), P(), P(), P(("blk", "group"))),
        out_specs=(rows, rows),
        check_vma=False,
    )
```

```python
import functools

import jax
import jax.numpy as jnp
from jax import lax
from jax.experimental import pallas as pl
from jax.experimental.pallas import tpu as pltpu
from jax.sharding import PartitionSpec as P

MESH = pl.DeviceIdType.MESH
SPAN = 4
OWN, AT_A, AT_C, AT_B = range(SPAN)
CHUNKS = 2
PARTS = 3
A, C, A2, C2 = range(0, 4 * CHUNKS, CHUNKS)
B, B2, X, M, X2 = range(4 * CHUNKS, 4 * CHUNKS + 5)
SEMS = 4 * CHUNKS + 5


def embed(feats, proj, loads):
    part = proj.shape[0] // PARTS
    x = 0.0
    for i, load in enumerate(loads):
        load.wait()
        here = slice(i * part, (i + 1) * part)
        x = x + jnp.dot(feats[:, here], proj[here, :], preferred_element_type=jnp.float32)
    inv = lax.rsqrt(jnp.sum(x * x, axis=-1, keepdims=True) + 1e-06)
    return x * inv, inv


def back_norm(grad, unit, inv, turned):
    inner = jnp.sum(grad * unit, axis=-1, keepdims=True)
    grad_x = (inv * (grad - inner * unit)).astype(jnp.bfloat16)
    out = jnp.dot(grad_x, turned, preferred_element_type=jnp.float32)
    return out.astype(jnp.bfloat16)


def kernel(
    n,
    image_feats, text_feats, image_proj, text_proj, matches, scale_ref, bias_ref,
    out,
    feats_i, feats_t, proj_i, proj_t, turned_i, turned_t,
    unit_i, inv_i, unit_t, inv_t, images, images_turned, texts, coefs, match, match_nbr,
    gi, gt_own, gt_a, send_a, send_b, send_c, send_x,
    got_a, got_b, got_c, got_x,
    load_sem, send_sem, recv_sem,
):
    rows = match.shape[1]
    step = rows // CHUNKS
    blk = lax.axis_index("blk")
    grp = lax.axis_index("group")
    odd = lax.rem(blk, 2)
    q = lax.rem(blk, 4)

    def at(distance):
        return lax.rem(blk + distance + n, n)

    sibling = blk + 1 - 2 * odd
    across = (blk, 1 - grp)
    from_a, from_b, from_c = at(-2), at(2 * odd - 3), at(-1 - 2 * odd)

    def load(src, dst, sem):
        return pltpu.make_async_copy(src, dst, load_sem.at[sem])

    def load_parts(src, dst, sem):
        part = src.shape[0] // PARTS
        return [
            load(src.at[pl.ds(i * part, part)], dst.at[pl.ds(i * part, part)], sem + i)
            for i in range(PARTS)
        ]

    def start(copies):
        for copy in copies:
            copy.start()

    load_t = load(text_feats, feats_t, 0)
    load_i = load(image_feats, feats_i, 1)
    load_m = load(matches, match, 2)
    loads_t = load_parts(text_proj, proj_t, 3)
    loads_i = load_parts(image_proj, proj_i, 3 + PARTS)
    load_t.start()
    start(loads_t)
    load_i.start()
    start(loads_i)
    load_m.start()

    barrier = pltpu.get_barrier_semaphore()

    def greet(partner):
        pl.semaphore_signal(barrier, inc=1, device_id=partner, device_id_type=MESH)

    greet((sibling, grp))
    greet(across)
    greet((at(6 * odd - 3), grp))
    greet((at(2), grp))
    greet((at(-2), grp))

    def remote(role, src, dst, partner):
        return pltpu.make_async_remote_copy(
            src_ref=src, dst_ref=dst, send_sem=send_sem.at[role],
            recv_sem=recv_sem.at[role], device_id=partner, device_id_type=MESH,
        )

    def part(i):
        return pl.ds(i * step, step)

    def between(role, src, dst, partner):
        return [
            remote(role + i, src.at[part(i)], dst.at[part(i)], partner)
            for i in range(CHUNKS)
        ]

    def wait_recv(copies):
        for copy in copies:
            copy.wait_recv()

    def wait_send(copies):
        for copy in copies:
            copy.wait_send()

    def slot(place):
        return texts.at[pl.ds(place * rows, rows)]

    load_t.wait()
    unit, inv = embed(feats_t, proj_t, loads_t)
    texts[:rows, :] = unit.astype(jnp.bfloat16)

    pl.semaphore_wait(barrier, 5)
    copy_a = between(A, slot(OWN), slot(AT_A), (at(2), grp))
    copy_b = remote(B, slot(OWN), slot(AT_B), (at(1 + 2 * odd), grp))
    copy_c = between(C, slot(AT_A), slot(AT_C), (sibling, grp))
    copy_m = remote(M, match, match_nbr, across)
    start(copy_a)
    pl.when(q != 3)(copy_b.start)
    load_m.wait()
    copy_m.start()
    unit_t[...] = unit
    inv_t[...] = inv

    load_i.wait()
    unit, inv = embed(feats_i, proj_i, loads_i)
    images[:rows, :] = unit.astype(jnp.bfloat16)
    copy_x = remote(X, images.at[pl.ds(0, rows)], images.at[pl.ds(rows, rows)], across)
    copy_x.start()
    unit_i[...] = unit
    inv_i[...] = inv

    scale = scale_ref[0]
    bias = bias_ref[0]

    def pair(place, source):
        ids = (source * 2 + grp) * rows + lax.broadcasted_iota(
            jnp.int32, (rows, 2 * rows), 0
        )
        wanted = jnp.concatenate([match[...], match_nbr[...]], axis=1)
        hit = wanted == ids
        here = slice(place * rows, (place + 1) * rows)
        logits = (
            scale
            * jnp.dot(texts[here, :], images_turned[...], preferred_element_type=jnp.float32)
            + bias
        )
        weight = jax.nn.sigmoid(jnp.where(hit, -logits, logits)) * scale
        coef = jnp.where(hit, -weight, weight).astype(jnp.bfloat16)
        coefs[here, :] = coef
        return jnp.dot(coef, images[...], preferred_element_type=jnp.float32)

    def image_terms():
        gi[...] = lax.dot_general(
            coefs[...], texts[...], (((0,), (0,)), ((), ())),
            preferred_element_type=jnp.float32,
        )
        send_x[...] = gi[rows:, :].astype(jnp.bfloat16)
        back_x.start()

    back_a = between(A2, send_a, got_a, (from_a, grp))
    back_b = remote(B2, send_b, got_b, (from_b, grp))
    back_c = between(C2, send_c, got_c, (sibling, grp))
    back_x = remote(X2, send_x, got_x, across)

    def pass_on(come, go):
        for i in range(CHUNKS):
            come[i].wait_recv()
            go[i].start()

    def finish_b():
        copy_b.wait_recv()
        send_b[...] = pair(AT_B, from_b).astype(jnp.bfloat16)
        back_b.start()

    def late_b():
        wait_send(copy_a)
        copy_b.start()

    pl.when(q == 3)(late_b)
    pass_on(copy_a, copy_c)
    copy_m.wait()
    copy_x.wait()
    images_turned[...] = images[...].T
    pl.when(odd == 1)(finish_b)
    gt_a[...] = pair(AT_A, from_a)
    gt_own[...] = pair(OWN, blk)

    wait_recv(copy_c)
    send_c[...] = pair(AT_C, from_c).astype(jnp.bfloat16)
    start(back_c)
    pl.when(odd == 0)(finish_b)
    pl.when(odd == 1)(image_terms)

    for i in range(CHUNKS):
        back_c[i].wait_recv()
        send_a[part(i), :] = (
            gt_a[part(i), :] + got_c[part(i), :].astype(jnp.float32)
        ).astype(jnp.bfloat16)
        back_a[i].start()

    pl.when(odd == 0)(image_terms)
    turned_i[...] = proj_i[...].T
    turned_t[...] = proj_t[...].T

    def finish_image():
        back_x.wait_recv()
        grad = gi[:rows, :] + got_x[...].astype(jnp.float32)
        out[:rows, :] = back_norm(grad, unit_i[...], inv_i[...], turned_i[...])

    def finish_text():
        back_b.wait_recv()
        gt_own[...] += got_b[...].astype(jnp.float32)
        wait_recv(back_a)
        grad = gt_own[...] + got_a[...].astype(jnp.float32)
        out[rows:, :] = back_norm(grad, unit_t[...], inv_t[...], turned_t[...])

    pl.when(blk < 2)(finish_text)
    finish_image()
    pl.when(blk >= 2)(finish_text)

    pl.when(q != 3)(lambda: wait_send(copy_a))
    for copies in ([copy_b], copy_c, back_a, [back_b], back_c, [back_x]):
        wait_send(copies)


def body(image_feats, text_feats, image_proj, text_proj, logit_scale, logit_bias, match):
    n = lax.axis_size("blk")
    rows, depth = image_feats.shape
    half = lambda *shape: pltpu.VMEM(shape, jnp.bfloat16)
    full = lambda *shape: pltpu.VMEM(shape, jnp.float32)
    far = pl.BlockSpec(memory_space=pltpu.HBM)
    near = pl.BlockSpec(memory_space=pltpu.VMEM)
    scalar = pl.BlockSpec(memory_space=pltpu.SMEM)
    tile = (rows, depth)
    both = pl.pallas_call(
        functools.partial(kernel, n),
        out_shape=jax.ShapeDtypeStruct((2 * rows, depth), jnp.bfloat16),
        in_specs=[far] * 5 + [scalar] * 2,
        out_specs=near,
        scratch_shapes=[
            half(*tile), half(*tile), half(depth, depth), half(depth, depth),
            half(depth, depth), half(depth, depth),
            full(*tile), full(rows, 1), full(*tile), full(rows, 1),
            half(2 * rows, depth), half(depth, 2 * rows),
            half(SPAN * rows, depth), half(SPAN * rows, 2 * rows),
            pltpu.VMEM((1, rows), jnp.int32), pltpu.VMEM((1, rows), jnp.int32),
            full(2 * rows, depth), full(*tile), full(*tile),
            half(*tile), half(*tile), half(*tile), half(*tile),
            half(*tile), half(*tile), half(*tile), half(*tile),
            pltpu.SemaphoreType.DMA((3 + 2 * PARTS,)),
            pltpu.SemaphoreType.DMA((SEMS,)),
            pltpu.SemaphoreType.DMA((SEMS,)),
        ],
        compiler_params=pltpu.CompilerParams(
            collective_id=0, has_side_effects=True, vmem_limit_bytes=32 * 1024 * 1024
        ),
        cost_estimate=pl.CostEstimate(
            flops=8 * rows * depth * depth + 48 * rows * rows * depth,
            bytes_accessed=4 * depth * depth + 8 * rows * depth,
            transcendentals=8 * rows * rows,
        ),
    )(
        *(
            pltpu.with_memory_space_constraint(x, pltpu.HBM)
            for x in (image_feats, text_feats, image_proj, text_proj, match.reshape(1, rows))
        ),
        logit_scale, logit_bias,
    )
    return both[:rows], both[rows:]


def solution(mesh):
    rows = P(("blk", "group"), None)
    return jax.shard_map(
        body,
        mesh=mesh,
        in_specs=(rows, rows, P(), P(), P(), P(), P(("blk", "group"))),
        out_specs=(rows, rows),
        check_vma=False,
    )
```

```python
import functools

import jax
import jax.numpy as jnp
from jax import lax
from jax.experimental import pallas as pl
from jax.experimental.pallas import tpu as pltpu
from jax.sharding import PartitionSpec as P

MESH = pl.DeviceIdType.MESH
SPAN = 4
OWN, AT_A, AT_C, AT_B = range(SPAN)
CHUNKS = 2
PARTS = 3
A, C, A2, C2 = range(0, 4 * CHUNKS, CHUNKS)
B, B2, X, M, X2 = range(4 * CHUNKS, 4 * CHUNKS + 5)
SEMS = 4 * CHUNKS + 5


def embed(feats, proj, loads):
    part = proj.shape[0] // PARTS
    x = 0.0
    for i, load in enumerate(loads):
        load.wait()
        here = slice(i * part, (i + 1) * part)
        x = x + jnp.dot(feats[:, here], proj[here, :], preferred_element_type=jnp.float32)
    inv = lax.rsqrt(jnp.sum(x * x, axis=-1, keepdims=True) + 1e-06)
    return x * inv, inv


def back_norm(grad, unit, inv, turned):
    inner = jnp.sum(grad * unit, axis=-1, keepdims=True)
    grad_x = (inv * (grad - inner * unit)).astype(jnp.bfloat16)
    out = jnp.dot(grad_x, turned, preferred_element_type=jnp.float32)
    return out.astype(jnp.bfloat16)


def kernel(
    n,
    image_feats, text_feats, image_proj, text_proj, matches, scale_ref, bias_ref,
    out,
    feats_i, feats_t, proj_i, proj_t, turned_i, turned_t,
    unit_i, inv_i, unit_t, inv_t, images, images_turned, texts, coefs, match, match_nbr,
    gi, gt_own, gt_a, send_a, send_b, send_c, send_x,
    got_a, got_b, got_c, got_x,
    load_sem, send_sem, recv_sem,
):
    rows = match.shape[1]
    step = rows // CHUNKS
    blk = lax.axis_index("blk")
    grp = lax.axis_index("group")
    odd = lax.rem(blk, 2)
    q = lax.rem(blk, 4)

    def at(distance):
        return lax.rem(blk + distance + n, n)

    sibling = blk + 1 - 2 * odd
    across = (blk, 1 - grp)
    from_a, from_b, from_c = at(-2), at(2 * odd - 3), at(-1 - 2 * odd)

    def load(src, dst, sem):
        return pltpu.make_async_copy(src, dst, load_sem.at[sem])

    def load_parts(src, dst, sem):
        part = src.shape[0] // PARTS
        return [
            load(src.at[pl.ds(i * part, part)], dst.at[pl.ds(i * part, part)], sem + i)
            for i in range(PARTS)
        ]

    def start(copies):
        for copy in copies:
            copy.start()

    load_t = load(text_feats, feats_t, 0)
    load_i = load(image_feats, feats_i, 1)
    load_m = load(matches, match, 2)
    loads_t = load_parts(text_proj, proj_t, 3)
    loads_i = load_parts(image_proj, proj_i, 3 + PARTS)
    load_t.start()
    start(loads_t)
    load_i.start()
    start(loads_i)
    load_m.start()

    barrier = pltpu.get_barrier_semaphore()

    def greet(partner):
        pl.semaphore_signal(barrier, inc=1, device_id=partner, device_id_type=MESH)

    greet((sibling, grp))
    greet(across)
    greet((at(6 * odd - 3), grp))
    greet((at(2), grp))
    greet((at(-2), grp))

    def remote(role, src, dst, partner):
        return pltpu.make_async_remote_copy(
            src_ref=src, dst_ref=dst, send_sem=send_sem.at[role],
            recv_sem=recv_sem.at[role], device_id=partner, device_id_type=MESH,
        )

    def part(i):
        return pl.ds(i * step, step)

    def between(role, src, dst, partner):
        return [
            remote(role + i, src.at[part(i)], dst.at[part(i)], partner)
            for i in range(CHUNKS)
        ]

    def wait_recv(copies):
        for copy in copies:
            copy.wait_recv()

    def wait_send(copies):
        for copy in copies:
            copy.wait_send()

    def slot(place):
        return texts.at[pl.ds(place * rows, rows)]

    load_t.wait()
    unit, inv = embed(feats_t, proj_t, loads_t)
    texts[:rows, :] = unit.astype(jnp.bfloat16)

    pl.semaphore_wait(barrier, 5)
    copy_a = between(A, slot(OWN), slot(AT_A), (at(2), grp))
    copy_b = remote(B, slot(OWN), slot(AT_B), (at(1 + 2 * odd), grp))
    copy_c = between(C, slot(AT_A), slot(AT_C), (sibling, grp))
    copy_m = remote(M, match, match_nbr, across)
    start(copy_a)
    pl.when(q != 3)(copy_b.start)
    load_m.wait()
    copy_m.start()
    unit_t[...] = unit
    inv_t[...] = inv

    load_i.wait()
    unit, inv = embed(feats_i, proj_i, loads_i)
    images[:rows, :] = unit.astype(jnp.bfloat16)
    copy_x = remote(X, images.at[pl.ds(0, rows)], images.at[pl.ds(rows, rows)], across)
    copy_x.start()
    unit_i[...] = unit
    inv_i[...] = inv

    scale = scale_ref[0]
    bias = bias_ref[0]

    def pair(place, source):
        ids = (source * 2 + grp) * rows + lax.broadcasted_iota(
            jnp.int32, (rows, 2 * rows), 0
        )
        wanted = jnp.concatenate([match[...], match_nbr[...]], axis=1)
        hit = wanted == ids
        here = slice(place * rows, (place + 1) * rows)
        logits = (
            scale
            * jnp.dot(texts[here, :], images_turned[...], preferred_element_type=jnp.float32)
            + bias
        )
        weight = jax.nn.sigmoid(jnp.where(hit, -logits, logits)) * scale
        coef = jnp.where(hit, -weight, weight).astype(jnp.bfloat16)
        coefs[here, :] = coef
        return jnp.dot(coef, images[...], preferred_element_type=jnp.float32)

    def image_terms():
        gi[...] = lax.dot_general(
            coefs[...], texts[...], (((0,), (0,)), ((), ())),
            preferred_element_type=jnp.float32,
        )
        send_x[...] = gi[rows:, :].astype(jnp.bfloat16)
        back_x.start()

    back_a = between(A2, send_a, got_a, (from_a, grp))
    back_b = remote(B2, send_b, got_b, (from_b, grp))
    back_c = between(C2, send_c, got_c, (sibling, grp))
    back_x = remote(X2, send_x, got_x, across)

    def pass_on(come, go):
        for i in range(CHUNKS):
            come[i].wait_recv()
            go[i].start()

    def finish_b():
        copy_b.wait_recv()
        send_b[...] = pair(AT_B, from_b).astype(jnp.bfloat16)
        pl.when(q != 0)(back_b.start)

    def late_b():
        wait_send(copy_a)
        copy_b.start()

    pl.when(q == 3)(late_b)
    pass_on(copy_a, copy_c)
    copy_m.wait()
    copy_x.wait()
    images_turned[...] = images[...].T
    pl.when(odd == 1)(finish_b)
    gt_a[...] = pair(AT_A, from_a)
    gt_own[...] = pair(OWN, blk)

    wait_recv(copy_c)
    send_c[...] = pair(AT_C, from_c).astype(jnp.bfloat16)
    start(back_c)
    pl.when(odd == 0)(finish_b)
    pl.when(odd == 1)(image_terms)

    for i in range(CHUNKS):
        back_c[i].wait_recv()
        send_a[part(i), :] = (
            gt_a[part(i), :] + got_c[part(i), :].astype(jnp.float32)
        ).astype(jnp.bfloat16)
        back_a[i].start()

    pl.when(q == 0)(back_b.start)
    pl.when(odd == 0)(image_terms)
    turned_i[...] = proj_i[...].T
    turned_t[...] = proj_t[...].T

    def finish_image():
        back_x.wait_recv()
        grad = gi[:rows, :] + got_x[...].astype(jnp.float32)
        out[:rows, :] = back_norm(grad, unit_i[...], inv_i[...], turned_i[...])

    def finish_text():
        back_b.wait_recv()
        gt_own[...] += got_b[...].astype(jnp.float32)
        wait_recv(back_a)
        grad = gt_own[...] + got_a[...].astype(jnp.float32)
        out[rows:, :] = back_norm(grad, unit_t[...], inv_t[...], turned_t[...])

    pl.when(blk < 2)(finish_text)
    finish_image()
    pl.when(blk >= 2)(finish_text)

    pl.when(q != 3)(lambda: wait_send(copy_a))
    for copies in ([copy_b], copy_c, back_a, [back_b], back_c, [back_x]):
        wait_send(copies)


def body(image_feats, text_feats, image_proj, text_proj, logit_scale, logit_bias, match):
    n = lax.axis_size("blk")
    rows, depth = image_feats.shape
    half = lambda *shape: pltpu.VMEM(shape, jnp.bfloat16)
    full = lambda *shape: pltpu.VMEM(shape, jnp.float32)
    far = pl.BlockSpec(memory_space=pltpu.HBM)
    near = pl.BlockSpec(memory_space=pltpu.VMEM)
    scalar = pl.BlockSpec(memory_space=pltpu.SMEM)
    tile = (rows, depth)
    both = pl.pallas_call(
        functools.partial(kernel, n),
        out_shape=jax.ShapeDtypeStruct((2 * rows, depth), jnp.bfloat16),
        in_specs=[far] * 5 + [scalar] * 2,
        out_specs=near,
        scratch_shapes=[
            half(*tile), half(*tile), half(depth, depth), half(depth, depth),
            half(depth, depth), half(depth, depth),
            full(*tile), full(rows, 1), full(*tile), full(rows, 1),
            half(2 * rows, depth), half(depth, 2 * rows),
            half(SPAN * rows, depth), half(SPAN * rows, 2 * rows),
            pltpu.VMEM((1, rows), jnp.int32), pltpu.VMEM((1, rows), jnp.int32),
            full(2 * rows, depth), full(*tile), full(*tile),
            half(*tile), half(*tile), half(*tile), half(*tile),
            half(*tile), half(*tile), half(*tile), half(*tile),
            pltpu.SemaphoreType.DMA((3 + 2 * PARTS,)),
            pltpu.SemaphoreType.DMA((SEMS,)),
            pltpu.SemaphoreType.DMA((SEMS,)),
        ],
        compiler_params=pltpu.CompilerParams(
            collective_id=0, has_side_effects=True, vmem_limit_bytes=32 * 1024 * 1024
        ),
        cost_estimate=pl.CostEstimate(
            flops=8 * rows * depth * depth + 48 * rows * rows * depth,
            bytes_accessed=4 * depth * depth + 8 * rows * depth,
            transcendentals=8 * rows * rows,
        ),
    )(
        *(
            pltpu.with_memory_space_constraint(x, pltpu.HBM)
            for x in (image_feats, text_feats, image_proj, text_proj, match.reshape(1, rows))
        ),
        logit_scale, logit_bias,
    )
    return both[:rows], both[rows:]


def solution(mesh):
    rows = P(("blk", "group"), None)
    return jax.shard_map(
        body,
        mesh=mesh,
        in_specs=(rows, rows, P(), P(), P(), P(), P(("blk", "group"))),
        out_specs=(rows, rows),
        check_vma=False,
    )
```

```python
import functools

import jax
import jax.numpy as jnp
from jax import lax
from jax.experimental import pallas as pl
from jax.experimental.pallas import tpu as pltpu
from jax.sharding import PartitionSpec as P

MESH = pl.DeviceIdType.MESH
SPAN = 4
OWN, AT_A, AT_C, AT_B = range(SPAN)
CHUNKS = 2
PARTS = 3
A, C, A2, B2, C2 = range(0, 5 * CHUNKS, CHUNKS)
B, X, M, X2 = range(5 * CHUNKS, 5 * CHUNKS + 4)
SEMS = 5 * CHUNKS + 4


def embed(feats, proj, loads):
    part = proj.shape[0] // PARTS
    x = 0.0
    for i, load in enumerate(loads):
        load.wait()
        here = slice(i * part, (i + 1) * part)
        x = x + jnp.dot(feats[:, here], proj[here, :], preferred_element_type=jnp.float32)
    inv = lax.rsqrt(jnp.sum(x * x, axis=-1, keepdims=True) + 1e-06)
    return x * inv, inv


def back_norm(grad, unit, inv, turned):
    inner = jnp.sum(grad * unit, axis=-1, keepdims=True)
    grad_x = (inv * (grad - inner * unit)).astype(jnp.bfloat16)
    out = jnp.dot(grad_x, turned, preferred_element_type=jnp.float32)
    return out.astype(jnp.bfloat16)


def kernel(
    n,
    image_feats, text_feats, image_proj, text_proj, matches, scale_ref, bias_ref,
    out,
    feats_i, feats_t, proj_i, proj_t, turned_i, turned_t,
    unit_i, inv_i, unit_t, inv_t, images, images_turned, texts, coefs, match, match_nbr,
    gi, gt_own, gt_a, send_a, send_b, send_c, send_x,
    got_a, got_b, got_c, got_x,
    load_sem, send_sem, recv_sem,
):
    rows = match.shape[1]
    step = rows // CHUNKS
    blk = lax.axis_index("blk")
    grp = lax.axis_index("group")
    odd = lax.rem(blk, 2)
    q = lax.rem(blk, 4)

    def at(distance):
        return lax.rem(blk + distance + n, n)

    sibling = blk + 1 - 2 * odd
    across = (blk, 1 - grp)
    from_a, from_b, from_c = at(-2), at(2 * odd - 3), at(-1 - 2 * odd)

    def load(src, dst, sem):
        return pltpu.make_async_copy(src, dst, load_sem.at[sem])

    def load_parts(src, dst, sem):
        part = src.shape[0] // PARTS
        return [
            load(src.at[pl.ds(i * part, part)], dst.at[pl.ds(i * part, part)], sem + i)
            for i in range(PARTS)
        ]

    def start(copies):
        for copy in copies:
            copy.start()

    load_t = load(text_feats, feats_t, 0)
    load_i = load(image_feats, feats_i, 1)
    load_m = load(matches, match, 2)
    loads_t = load_parts(text_proj, proj_t, 3)
    loads_i = load_parts(image_proj, proj_i, 3 + PARTS)
    load_t.start()
    start(loads_t)
    load_i.start()
    start(loads_i)
    load_m.start()

    barrier = pltpu.get_barrier_semaphore()

    def greet(partner):
        pl.semaphore_signal(barrier, inc=1, device_id=partner, device_id_type=MESH)

    greet((sibling, grp))
    greet(across)
    greet((at(6 * odd - 3), grp))
    greet((at(2), grp))
    greet((at(-2), grp))

    def remote(role, src, dst, partner):
        return pltpu.make_async_remote_copy(
            src_ref=src, dst_ref=dst, send_sem=send_sem.at[role],
            recv_sem=recv_sem.at[role], device_id=partner, device_id_type=MESH,
        )

    def part(i):
        return pl.ds(i * step, step)

    def between(role, src, dst, partner):
        return [
            remote(role + i, src.at[part(i)], dst.at[part(i)], partner)
            for i in range(CHUNKS)
        ]

    def wait_recv(copies):
        for copy in copies:
            copy.wait_recv()

    def wait_send(copies):
        for copy in copies:
            copy.wait_send()

    def slot(place):
        return texts.at[pl.ds(place * rows, rows)]

    load_t.wait()
    unit, inv = embed(feats_t, proj_t, loads_t)
    texts[:rows, :] = unit.astype(jnp.bfloat16)

    pl.semaphore_wait(barrier, 5)
    copy_a = between(A, slot(OWN), slot(AT_A), (at(2), grp))
    copy_b = remote(B, slot(OWN), slot(AT_B), (at(1 + 2 * odd), grp))
    copy_c = between(C, slot(AT_A), slot(AT_C), (sibling, grp))
    copy_m = remote(M, match, match_nbr, across)
    start(copy_a)
    pl.when(q != 3)(copy_b.start)
    load_m.wait()
    copy_m.start()
    unit_t[...] = unit
    inv_t[...] = inv

    load_i.wait()
    unit, inv = embed(feats_i, proj_i, loads_i)
    images[:rows, :] = unit.astype(jnp.bfloat16)
    copy_x = remote(X, images.at[pl.ds(0, rows)], images.at[pl.ds(rows, rows)], across)
    copy_x.start()
    unit_i[...] = unit
    inv_i[...] = inv

    scale = scale_ref[0]
    bias = bias_ref[0]

    def pair(place, source):
        ids = (source * 2 + grp) * rows + lax.broadcasted_iota(
            jnp.int32, (rows, 2 * rows), 0
        )
        wanted = jnp.concatenate([match[...], match_nbr[...]], axis=1)
        hit = wanted == ids
        here = slice(place * rows, (place + 1) * rows)
        logits = (
            scale
            * jnp.dot(texts[here, :], images_turned[...], preferred_element_type=jnp.float32)
            + bias
        )
        weight = jax.nn.sigmoid(jnp.where(hit, -logits, logits)) * scale
        coef = jnp.where(hit, -weight, weight).astype(jnp.bfloat16)
        coefs[here, :] = coef
        return jnp.dot(coef, images[...], preferred_element_type=jnp.float32)

    def image_terms():
        gi[...] = lax.dot_general(
            coefs[...], texts[...], (((0,), (0,)), ((), ())),
            preferred_element_type=jnp.float32,
        )
        send_x[...] = gi[rows:, :].astype(jnp.bfloat16)
        back_x.start()

    back_a = between(A2, send_a, got_a, (from_a, grp))
    back_b = between(B2, send_b, got_b, (from_b, grp))
    back_c = between(C2, send_c, got_c, (sibling, grp))
    back_x = remote(X2, send_x, got_x, across)

    def pass_on(come, go):
        for i in range(CHUNKS):
            come[i].wait_recv()
            go[i].start()

    def finish_b():
        copy_b.wait_recv()
        send_b[...] = pair(AT_B, from_b).astype(jnp.bfloat16)
        back_b[0].start()
        pl.when(q != 0)(lambda: start(back_b[1:]))

    def late_b():
        wait_send(copy_a)
        copy_b.start()

    pl.when(q == 3)(late_b)
    pass_on(copy_a, copy_c)
    copy_m.wait()
    copy_x.wait()
    images_turned[...] = images[...].T
    pl.when(odd == 1)(finish_b)
    gt_a[...] = pair(AT_A, from_a)
    gt_own[...] = pair(OWN, blk)

    wait_recv(copy_c)
    send_c[...] = pair(AT_C, from_c).astype(jnp.bfloat16)
    start(back_c)
    pl.when(odd == 0)(finish_b)
    image_terms()

    for i in range(CHUNKS):
        back_c[i].wait_recv()
        send_a[part(i), :] = (
            gt_a[part(i), :] + got_c[part(i), :].astype(jnp.float32)
        ).astype(jnp.bfloat16)
        back_a[i].start()

    pl.when(q == 0)(lambda: start(back_b[1:]))
    turned_i[...] = proj_i[...].T
    turned_t[...] = proj_t[...].T

    def finish_image():
        back_x.wait_recv()
        grad = gi[:rows, :] + got_x[...].astype(jnp.float32)
        out[:rows, :] = back_norm(grad, unit_i[...], inv_i[...], turned_i[...])

    def finish_text():
        wait_recv(back_b)
        gt_own[...] += got_b[...].astype(jnp.float32)
        wait_recv(back_a)
        grad = gt_own[...] + got_a[...].astype(jnp.float32)
        out[rows:, :] = back_norm(grad, unit_t[...], inv_t[...], turned_t[...])

    pl.when(blk < 2)(finish_text)
    finish_image()
    pl.when(blk >= 2)(finish_text)

    pl.when(q != 3)(lambda: wait_send(copy_a))
    for copies in ([copy_b], copy_c, back_a, back_b, back_c, [back_x]):
        wait_send(copies)


def body(image_feats, text_feats, image_proj, text_proj, logit_scale, logit_bias, match):
    n = lax.axis_size("blk")
    rows, depth = image_feats.shape
    half = lambda *shape: pltpu.VMEM(shape, jnp.bfloat16)
    full = lambda *shape: pltpu.VMEM(shape, jnp.float32)
    far = pl.BlockSpec(memory_space=pltpu.HBM)
    near = pl.BlockSpec(memory_space=pltpu.VMEM)
    scalar = pl.BlockSpec(memory_space=pltpu.SMEM)
    tile = (rows, depth)
    both = pl.pallas_call(
        functools.partial(kernel, n),
        out_shape=jax.ShapeDtypeStruct((2 * rows, depth), jnp.bfloat16),
        in_specs=[far] * 5 + [scalar] * 2,
        out_specs=near,
        scratch_shapes=[
            half(*tile), half(*tile), half(depth, depth), half(depth, depth),
            half(depth, depth), half(depth, depth),
            full(*tile), full(rows, 1), full(*tile), full(rows, 1),
            half(2 * rows, depth), half(depth, 2 * rows),
            half(SPAN * rows, depth), half(SPAN * rows, 2 * rows),
            pltpu.VMEM((1, rows), jnp.int32), pltpu.VMEM((1, rows), jnp.int32),
            full(2 * rows, depth), full(*tile), full(*tile),
            half(*tile), half(*tile), half(*tile), half(*tile),
            half(*tile), half(*tile), half(*tile), half(*tile),
            pltpu.SemaphoreType.DMA((3 + 2 * PARTS,)),
            pltpu.SemaphoreType.DMA((SEMS,)),
            pltpu.SemaphoreType.DMA((SEMS,)),
        ],
        compiler_params=pltpu.CompilerParams(
            collective_id=0, has_side_effects=True, vmem_limit_bytes=32 * 1024 * 1024
        ),
        cost_estimate=pl.CostEstimate(
            flops=8 * rows * depth * depth + 48 * rows * rows * depth,
            bytes_accessed=4 * depth * depth + 8 * rows * depth,
            transcendentals=8 * rows * rows,
        ),
    )(
        *(
            pltpu.with_memory_space_constraint(x, pltpu.HBM)
            for x in (image_feats, text_feats, image_proj, text_proj, match.reshape(1, rows))
        ),
        logit_scale, logit_bias,
    )
    return both[:rows], both[rows:]


def solution(mesh):
    rows = P(("blk", "group"), None)
    return jax.shard_map(
        body,
        mesh=mesh,
        in_specs=(rows, rows, P(), P(), P(), P(), P(("blk", "group"))),
        out_specs=(rows, rows),
        check_vma=False,
    )
```
